256 devices in a mesh: band: 32 (over z, x_hi, core), kpt: 8 (over x_lo, y).
Axes of the slice: x: 4 (x_hi: 2, x_lo: 2; x = x_hi * 2 + x_lo), y: 4, z: 8, core: 2. Of those that a mesh axis runs over, the one named last changes fastest.
Arguments:
- orbitals: bfloat16 [8, 32, 2, 64000], P('kpt', 'band'), may hold values from -6 to 6
- coulomb: float32 [8, 2, 64000], P('kpt'), may hold values from 0.1 to 2
Outputs:
- exchange: float32 [8, 32, 2, 64000], P('kpt', 'band')
The draws below stay inside these ranges and needn't reach their ends.
All inputs are finite; a program needn't handle non-finite values.
Results may differ from the reference program's by a relative error of at most 0.0085.
Values may be sent and summed in bfloat16 or wider, within the bound.
A program may use at most 64 MiB of HBM per device.

```python
import math
import jax
import jax.numpy as jnp
from jax import lax

NG = 40
NB = 1
KSTEPS = 2
BSTEPS = 2
GRID = 64000
NBLOCK = 32
NBAND = 32
NK = 8


def steps_of(key, dims, shards, low, largest):
    level = 1.0
    for axis_at, blocks in shards:
        steps = jax.random.uniform(jax.random.fold_in(jax.random.fold_in(key, 6), axis_at), (blocks,), jnp.float32, low / len(shards), largest / len(shards))
        level = level * jnp.repeat(jnp.exp(steps), dims[axis_at] // blocks).reshape((-1,) + (1,) * (len(dims) - 1 - axis_at))
    return level


def centred(stream_key, extent, width, limit, pieces=(), kind=jnp.bfloat16):
    factor_of = steps_of(stream_key, extent, pieces, -0.22, 0.18) if pieces else 1.0
    values = jax.random.normal(stream_key, extent, jnp.float32) * width * factor_of
    return jnp.minimum(jnp.maximum(values, -limit), limit).astype(kind)


def setup_inputs(seed: int = 0) -> dict:
    key_of = jax.random.split(jax.random.key(seed), 3)
    return {
        "orbitals": centred(key_of[0], (NK, NBAND, 2, GRID), 1.0, 6.0, ((0, 8), (1, 32))),
        "coulomb": jnp.clip(jnp.exp(math.log(2.0) - 2.9957323 * jax.random.uniform(key_of[1], (NK, KSTEPS, GRID), jnp.float32) ** steps_of(key_of[1], (NK, KSTEPS, GRID), ((0, 8),), -0.2, 0.2)), 0.1, 2.0),
    }


def fourier_tables(size):
    points = jnp.arange(size, dtype=jnp.int32)
    phase = points[:, None] * points[None, :] % size
    angle = phase.astype(jnp.float32) * (2.0 * math.pi / size)
    factor = 1.0 / math.sqrt(size)
    cosine = (jnp.cos(angle) * factor).astype(jnp.bfloat16)
    sine = (jnp.sin(angle) * factor).astype(jnp.bfloat16)
    forward = jnp.concatenate([jnp.concatenate([cosine, sine], 1), jnp.concatenate([-sine, cosine], 1)], 0)
    inverse = jnp.concatenate([jnp.concatenate([cosine, -sine], 1), jnp.concatenate([sine, cosine], 1)], 0)
    return (forward, inverse)

def rounded(values):
    return lax.optimization_barrier(values.astype(jnp.bfloat16)).astype(jnp.float32)

def one_pass(table, field):
    size = table.shape[0] // 2
    count = field.shape[0]
    result = jnp.einsum('ij,pjk->pik', table, field, precision=lax.Precision.HIGHEST)
    result = result.reshape(count, 2, size, size, size).transpose(0, 1, 3, 4, 2)
    return result.reshape(count, 2 * size, size * size)

def potential(own_block, visiting, kernel_row, forward, inverse):
    bands = own_block.shape[0]
    size = forward.shape[0] // 2
    points = own_block.shape[2]
    own_re, own_im = (own_block[:, 0], own_block[:, 1])
    vis_re, vis_im = (visiting[:, 0], visiting[:, 1])
    dens_re = own_re[:, None] * vis_re[None] + own_im[:, None] * vis_im[None]
    dens_im = own_im[:, None] * vis_re[None] - own_re[:, None] * vis_im[None]
    count = bands * bands
    field = rounded(jnp.stack([dens_re, dens_im], 2).reshape(count, 2 * size, size * size))
    for repeat in range(3):
        field = rounded(one_pass(forward, field))
    field = rounded(field.reshape(count, 2, points) * kernel_row[None, None, :]).reshape(count, 2 * size, size * size)
    for repeat in range(2):
        field = rounded(one_pass(inverse, field))
    field = one_pass(inverse, field)
    wave = field.reshape(bands, bands, 2, points)
    w_re, w_im = (wave[:, :, 0], wave[:, :, 1])
    term_re = lax.optimization_barrier(jnp.sum(vis_re[None] * w_re - vis_im[None] * w_im, axis=1))
    term_im = lax.optimization_barrier(jnp.sum(vis_re[None] * w_im + vis_im[None] * w_re, axis=1))
    return jnp.stack([term_re, term_im], 1)

def starts(*values):
    return tuple((jnp.asarray(value).astype(jnp.int32) for value in values))

def reference(orbitals, coulomb):
    forward, inverse = fourier_tables(NG)
    forward = forward.astype(jnp.float32)
    inverse = inverse.astype(jnp.float32)
    weight = -1.0 / (KSTEPS * (BSTEPS + 1) * NB)

    def one_block(flat_index):
        kpoint = (flat_index // NBLOCK).astype(jnp.int32)
        block = (flat_index % NBLOCK).astype(jnp.int32)
        own_block = lax.dynamic_slice(orbitals, starts(kpoint, block * NB, 0, 0), (1, NB, 2, GRID))[0].astype(jnp.float32)
        total = jnp.zeros((NB, 2, GRID), jnp.float32)
        for k_step in range(KSTEPS):
            other = ((kpoint - k_step) % NK).astype(jnp.int32)
            kernel_row = lax.dynamic_slice(coulomb, starts(kpoint, k_step, 0), (1, 1, GRID))[0, 0]
            for cycle_step in range(BSTEPS + 1):
                source = ((block - cycle_step) % NBLOCK).astype(jnp.int32)
                visiting = lax.dynamic_slice(orbitals, starts(other, source * NB, 0, 0), (1, NB, 2, GRID))[0].astype(jnp.float32)
                total = total + potential(own_block, visiting, kernel_row, forward, inverse)
        return total * weight
    blocks = lax.map(one_block, jnp.arange(NK * NBLOCK, dtype=jnp.int32))
    return blocks.reshape(NK, NBAND, 2, GRID)
```

```python
import math

import jax
import jax.numpy as jnp
import ml_dtypes
import numpy as np
from jax import lax
from jax.experimental import pallas as pl
from jax.experimental.pallas import tpu as pltpu
from jax.sharding import PartitionSpec as P

NG = 40
KSTEPS = 2
BSTEPS = 2
TERMS = BSTEPS + 1
NBLOCK = 32
NK = 8
WEIGHT = -1.0 / (KSTEPS * TERMS)
BF16 = jnp.bfloat16
F32 = jnp.float32
MESH = pl.DeviceIdType.MESH
TILES = 13
ROWS = TILES * 128
CHUNKS = ((0, 7), (7, 6))


def tables():
    points = np.arange(NG)
    angle = (points[:, None] * points[None, :] % NG) * (2.0 * math.pi / NG)
    scale = 1.0 / math.sqrt(NG)
    c, s = (
        (f(angle) * scale).astype(ml_dtypes.bfloat16).astype(np.float32) for f in (np.cos, np.sin)
    )
    first = np.zeros((TERMS, 2, NG, 2, 128), np.float32)
    last = np.zeros((TERMS, 2, NG, 2, 128), np.float32)
    for t in range(TERMS):
        lanes = slice(NG * t, NG * t + NG)
        first[t, 0, :, 0, lanes] = c
        first[t, 1, :, 0, lanes] = s
        first[t, 0, :, 1, lanes] = -s
        first[t, 1, :, 1, lanes] = c
        last[t, 0, :, 0, lanes] = c
        last[t, 0, :, 1, lanes] = -s
        last[t, 1, :, 1, lanes] = c
        last[t, 1, :, 0, lanes] = s

    def rows(sign):
        table = np.zeros((2, 2, NG, 2, 2, NG), np.float32)
        for i in range(2):
            table[0, i, :, 0, i, :] = c
            table[0, i, :, 1, i, :] = sign * s
            table[1, i, :, 0, i, :] = -sign * s
            table[1, i, :, 1, i, :] = c
        return np.pad(table.reshape(160, 160), ((0, 0), (0, 96)))

    spread = np.zeros((2, 2, NG, 2, 128), np.float32)
    for s_at in range(2):
        for t in range(TERMS):
            for half in range(2):
                spread[half, s_at, points, s_at, NG * t + points] = 1
    parts = [first.reshape(240, 256), last.reshape(240, 256), rows(1.0), rows(-1.0), spread.reshape(160, 256)]
    return np.concatenate(parts, 0).astype(ml_dtypes.bfloat16)


def matrix_from_flat(flat, matrix, odd):
    for a in range(NG // 2):
        for j in range(25):
            at = 128 * (25 * a + j)
            tile = flat[:, at : at + 128].astype(F32)
            if j <= 12:
                matrix[j, pl.ds(2 * a, 2, stride=NG), :] = tile
            if j >= 12:
                odd[j - 12, pl.ds(a, 2, stride=24), :] = tile
    lane = lax.broadcasted_iota(jnp.int32, (NG // 2, 128), 1)
    for c in range(2):
        here = pltpu.roll(odd[0, 24 * c : 24 * c + 20, :], 64, 1)
        for j in range(TILES):
            after = pltpu.roll(odd[j + 1, 24 * c : 24 * c + 20, :], 64, 1) if j < 12 else here
            matrix[j, pl.ds(NG * c + 1, 20, stride=2), :] = jnp.where(lane < 64, here, after)
            here = after


def flat_from_matrix(matrix, flat, odd):
    lane = lax.broadcasted_iota(jnp.int32, (NG // 2, 128), 1)
    for c in range(2):
        before = matrix[12, pl.ds(NG * c, 20, stride=2), :]
        for j in range(TILES):
            here = pltpu.roll(matrix[j, pl.ds(NG * c + 1, 20, stride=2), :], 64, 1)
            odd[j, 24 * c : 24 * c + 20, :] = jnp.where(lane < 64, before, here)
            before = here
    for a in range(NG // 2):
        for j in range(25):
            at = 128 * (25 * a + j)
            flat[:, at : at + 128] = (
                matrix[j, pl.ds(2 * a, 2, stride=NG), :] if j < 12 else odd[j - 12, pl.ds(a, 2, stride=24), :]
            )


def dot(a, b, on):
    return lax.dot_general(a, b, ((on[:1], on[1:]), ((), ())), preferred_element_type=F32)


def spread_coulomb(matrix, spread, out):
    for j in range(TILES):
        value = matrix[j]
        high = value.astype(BF16)
        low = (value - high.astype(F32)).astype(BF16)
        both = dot(jnp.concatenate([high, low], 0), spread, (0, 0))
        out[0, 128 * j : 128 * j + 128, :] = both[:, :128]
        out[1, 128 * j : 128 * j + 128, :] = both[:, 128:]


def terms(own, visiting, coulomb, tab, total, first, fa, fb, fc, fd):
    table = lambda at, rows, cols=256: tab[at : at + rows, :cols]
    for j in range(TILES):
        a = own[j].astype(F32)
        a_re, a_im = a[:NG], a[NG:]
        parts = []
        for ref in visiting:
            b = ref[j].astype(F32)
            b_re, b_im = b[:NG], b[NG:]
            parts += [a_re * b_re + a_im * b_im, a_im * b_re - a_re * b_im]
        density = jnp.concatenate(parts, 0).astype(BF16)
        fa[128 * j : 128 * j + 128, :] = dot(density, table(0, 240), (0, 0)).astype(BF16)
    forward, inverse = table(480, 160, 160), table(640, 160, 160)
    for i in range(10):
        at = 160 * i
        a, b = fa[at : at + 80, :], fa[at + 80 : at + 160, :]
        field = jnp.concatenate(
            [jnp.concatenate([a[:, :128], b[:, :128]], 1), jnp.concatenate([a[:, 128:], b[:, 128:]], 1)], 0
        )
        r = dot(forward, field, (1, 0))
        for c in range(2):
            fb[c, at : at + 80, :] = r[80 * c : 80 * c + 80, :128]
            fb[c, at + 80 : at + 160, :] = r[80 * c : 80 * c + 80, 128:]
    for i in range(10):
        halves, scales = [], []
        for h in range(2):
            z = 4 * i + 2 * h
            halves.append(
                jnp.concatenate([fb[c, pl.ds(z + q, NG, stride=NG), :] for c in range(2) for q in range(2)], 0)
            )
            scales.append(jnp.concatenate([coulomb[pl.ds(z + q, NG, stride=NG), :] for q in range(2)] * 2, 0))
        field = jnp.concatenate(halves, 1).astype(BF16)
        r = dot(forward, field, (1, 0)).astype(BF16).astype(F32)
        scaled = (r * jnp.concatenate(scales, 1)).astype(BF16)
        r = dot(inverse, scaled, (1, 0))
        for h in range(2):
            for c in range(2):
                for q in range(2):
                    at = 80 * c + NG * q
                    fc[c, pl.ds(4 * i + 2 * h + q, NG, stride=NG), :] = r[at : at + NG, 128 * h : 128 * h + 128]
    for i in range(10):
        at = 160 * i
        field = jnp.concatenate(
            [jnp.concatenate([fc[c, at : at + 80, :], fc[c, at + 80 : at + 160, :]], 1) for c in range(2)], 0
        ).astype(BF16)
        r = dot(inverse, field, (1, 0)).astype(BF16)
        fd[at : at + 80, :] = jnp.concatenate([r[:80, :128], r[80:, :128]], 1)
        fd[at + 80 : at + 160, :] = jnp.concatenate([r[:80, 128:], r[80:, 128:]], 1)
    for j in range(TILES):
        wave = dot(table(240, 240), fd[128 * j : 128 * j + 128, :], (1, 1))
        re = im = 0.0
        for t, ref in enumerate(visiting):
            b = ref[j].astype(F32)
            b_re, b_im = b[:NG], b[NG:]
            w_re, w_im = wave[80 * t : 80 * t + NG], wave[80 * t + NG : 80 * t + 80]
            re = re + (b_re * w_re - b_im * w_im)
            im = im + (b_re * w_im + b_im * w_re)
        value = jnp.concatenate([re, im], 0)
        total[j] = value if first else (total[j] + value) * WEIGHT


def kernel(
    orbitals, coulomb, tables_ref, out,
    flat, kernel_flat, tab, matrix, kernel_matrix, odd, own, vis, total, scale, fa, fb, fc, fd, out_flat,
    local_sem, send_sem, recv_sem,
):
    n, k = lax.axis_index("band"), lax.axis_index("kpt")
    core = lax.rem(n, 2)
    sibling = n + 1 - 2 * core
    behind, ahead = lax.rem(n + NBLOCK - 2, NBLOCK), lax.rem(n + 2, NBLOCK)
    k_behind, k_ahead = lax.rem(k + NK - 1, NK), lax.rem(k + 1, NK)
    turns, turned = lax.rem(k, 4) == 3, lax.rem(k, 4) == 0

    loads = [
        pltpu.make_async_copy(orbitals.at[0, 0], flat, local_sem.at[0]),
        pltpu.make_async_copy(coulomb.at[0], kernel_flat, local_sem.at[1]),
        pltpu.make_async_copy(tables_ref, tab, local_sem.at[2]),
    ]
    for load in loads:
        load.start()
    barrier = pltpu.get_barrier_semaphore()
    for peer in ((behind, k), (n, k_behind), (sibling, k), (behind, k_behind)):
        pl.semaphore_signal(barrier, inc=1, device_id=peer, device_id_type=MESH)
    loads[0].wait()
    matrix_from_flat(flat, matrix, odd)
    own[...] = matrix[...].astype(BF16)
    pl.semaphore_wait(barrier, 4)

    used = [0]

    def copy(src, dst, peer):
        at = used[0]
        used[0] += 1
        return pltpu.make_async_remote_copy(
            src_ref=src, dst_ref=dst, send_sem=send_sem.at[at], recv_sem=recv_sem.at[at],
            device_id=peer, device_id_type=MESH,
        )

    def chunk(ref, c):
        return ref.at[pl.ds(c[0], c[1])]

    to_ahead = [copy(chunk(own, c), chunk(vis.at[0], c), (ahead, k)) for c in CHUNKS]
    to_next_k = copy(own, vis.at[2], (n, k_ahead))
    turn = copy(own, vis.at[3], (ahead, k_ahead))
    on = [copy(chunk(vis.at[0], c), chunk(vis.at[3], c), (n, k_ahead)) for c in CHUNKS]
    even_own = copy(own, vis.at[1], (sibling, k))
    even_partner = copy(vis.at[2], vis.at[4], (sibling, k))
    odd_own = [copy(chunk(vis.at[0], c), chunk(vis.at[1], c), (sibling, k)) for c in CHUNKS]
    odd_partner = [copy(chunk(vis.at[3], c), chunk(vis.at[4], c), (sibling, k)) for c in CHUNKS]

    def when(flag, *steps):
        @pl.when(flag)
        def _():
            for step in steps:
                step()

    for c in to_ahead:
        c.start()
    to_next_k.start()
    when(turns, turn.start)
    when(core == 0, even_own.start)
    loads[1].wait()
    matrix_from_flat(kernel_flat, kernel_matrix, odd)
    loads[2].wait()
    spread_coulomb(kernel_matrix, tab[800:960, :], scale)
    for i in range(2):
        to_ahead[i].wait_recv()
        when(jnp.logical_not(turns), on[i].start)
        when(core == 1, odd_own[i].start)
    to_next_k.wait_recv()
    when(core == 0, even_partner.start)
    when(core == 0, *[c.wait_recv for c in odd_own])
    when(core == 1, even_own.wait_recv)
    terms(own, [own, vis.at[1], vis.at[0]], scale.at[0], tab, total, True, fa, fb, fc, fd)
    when(turned, turn.wait_recv)
    for i in range(2):
        when(jnp.logical_not(turned), on[i].wait_recv)
        when(core == 1, odd_partner[i].start)
    when(core == 0, *[c.wait_recv for c in odd_partner])
    when(core == 1, even_partner.wait_recv)
    terms(own, [vis.at[2], vis.at[4], vis.at[3]], scale.at[1], tab, total, False, fa, fb, fc, fd)
    flat_from_matrix(total, out_flat, odd)
    store = pltpu.make_async_copy(out_flat, out.at[0, 0], local_sem.at[0])
    store.start()
    for c in to_ahead:
        c.wait_send()
    to_next_k.wait_send()
    when(turns, turn.wait_send)
    when(jnp.logical_not(turns), *[c.wait_send for c in on])
    when(core == 0, even_own.wait_send, even_partner.wait_send)
    when(core == 1, *[c.wait_send for c in odd_own + odd_partner])
    store.wait()


def shards(orbitals, coulomb):
    field = (TILES, 2 * NG, 128)
    vmem = pltpu.VMEM
    return pl.pallas_call(
        kernel,
        out_shape=jax.ShapeDtypeStruct(orbitals.shape, F32),
        in_specs=[pl.BlockSpec(memory_space=pl.ANY)] * 3,
        out_specs=pl.BlockSpec(memory_space=pl.ANY),
        scratch_shapes=[
            vmem((2, 64000), BF16), vmem((2, 64000), F32), vmem((960, 256), BF16), vmem(field, F32), vmem(field, F32),
            vmem((14, 48, 128), F32), vmem(field, BF16), vmem((5, *field), BF16), vmem(field, F32), vmem((2, ROWS, 128), F32),
            vmem((ROWS, 256), BF16), vmem((2, 1600, 128), F32), vmem((2, 1600, 128), F32), vmem((ROWS, 256), BF16),
            vmem((2, 64000), F32), pltpu.SemaphoreType.DMA((3,)), pltpu.SemaphoreType.DMA((16,)), pltpu.SemaphoreType.DMA((16,)),
        ],
        compiler_params=pltpu.CompilerParams(collective_id=0, has_side_effects=True, vmem_limit_bytes=56 << 20),
    )(orbitals, coulomb, jnp.asarray(tables()))


def solution(mesh):
    return jax.shard_map(
        shards,
        mesh=mesh,
        in_specs=(P("kpt", "band", None, None), P("kpt", None, None)),
        out_specs=P("kpt", "band", None, None),
        check_vma=False,
    )
```

```python
import math

import jax
import jax.numpy as jnp
import ml_dtypes
import numpy as np
from jax import lax
from jax.experimental import pallas as pl
from jax.experimental.pallas import tpu as pltpu
from jax.sharding import PartitionSpec as P

NG = 40
KSTEPS = 2
BSTEPS = 2
TERMS = BSTEPS + 1
NBLOCK = 32
NK = 8
WEIGHT = -1.0 / (KSTEPS * TERMS)
BF16 = jnp.bfloat16
F32 = jnp.float32
MESH = pl.DeviceIdType.MESH
TILES = 13
ROWS = TILES * 128
CHUNKS = ((0, 7), (7, 6))


def tables():
    points = np.arange(NG)
    angle = (points[:, None] * points[None, :] % NG) * (2.0 * math.pi / NG)
    scale = 1.0 / math.sqrt(NG)
    c, s = (
        (f(angle) * scale).astype(ml_dtypes.bfloat16).astype(np.float32) for f in (np.cos, np.sin)
    )
    first = np.zeros((TERMS, 2, NG, 2, 128), np.float32)
    last = np.zeros((TERMS, 2, NG, 2, 128), np.float32)
    for t in range(TERMS):
        lanes = slice(NG * t, NG * t + NG)
        first[t, 0, :, 0, lanes] = c
        first[t, 1, :, 0, lanes] = s
        first[t, 0, :, 1, lanes] = -s
        first[t, 1, :, 1, lanes] = c
        last[t, 0, :, 0, lanes] = c
        last[t, 0, :, 1, lanes] = -s
        last[t, 1, :, 1, lanes] = c
        last[t, 1, :, 0, lanes] = s

    def rows(sign):
        table = np.zeros((2, 2, NG, 2, 2, NG), np.float32)
        for i in range(2):
            table[0, i, :, 0, i, :] = c
            table[0, i, :, 1, i, :] = sign * s
            table[1, i, :, 0, i, :] = -sign * s
            table[1, i, :, 1, i, :] = c
        return np.pad(table.reshape(160, 160), ((0, 0), (0, 96)))

    spread = np.zeros((2, 2, NG, 2, 128), np.float32)
    for s_at in range(2):
        for t in range(TERMS):
            for half in range(2):
                spread[half, s_at, points, s_at, NG * t + points] = 1
    parts = [first.reshape(240, 256), last.reshape(240, 256), rows(1.0), rows(-1.0), spread.reshape(160, 256)]
    return np.concatenate(parts, 0).astype(ml_dtypes.bfloat16)


def matrix_from_flat(flat, matrix, odd):
    for a in range(NG // 2):
        for j in range(25):
            at = 128 * (25 * a + j)
            tile = flat[:, at : at + 128].astype(F32)
            if j <= 12:
                matrix[j, pl.ds(2 * a, 2, stride=NG), :] = tile
            if j >= 12:
                odd[j - 12, pl.ds(a, 2, stride=24), :] = tile
    lane = lax.broadcasted_iota(jnp.int32, (NG // 2, 128), 1)
    for c in range(2):
        here = pltpu.roll(odd[0, 24 * c : 24 * c + 20, :], 64, 1)
        for j in range(TILES):
            after = pltpu.roll(odd[j + 1, 24 * c : 24 * c + 20, :], 64, 1) if j < 12 else here
            matrix[j, pl.ds(NG * c + 1, 20, stride=2), :] = jnp.where(lane < 64, here, after)
            here = after


def flat_from_matrix(matrix, flat, odd):
    lane = lax.broadcasted_iota(jnp.int32, (NG // 2, 128), 1)
    for c in range(2):
        before = matrix[12, pl.ds(NG * c, 20, stride=2), :]
        for j in range(TILES):
            here = pltpu.roll(matrix[j, pl.ds(NG * c + 1, 20, stride=2), :], 64, 1)
            odd[j, 24 * c : 24 * c + 20, :] = jnp.where(lane < 64, before, here)
            before = here
    for a in range(NG // 2):
        for j in range(25):
            at = 128 * (25 * a + j)
            flat[:, at : at + 128] = (
                matrix[j, pl.ds(2 * a, 2, stride=NG), :] if j < 12 else odd[j - 12, pl.ds(a, 2, stride=24), :]
            )


def dot(a, b, on):
    return lax.dot_general(a, b, ((on[:1], on[1:]), ((), ())), preferred_element_type=F32)


def spread_coulomb(matrix, spread, out):
    for j in range(TILES):
        value = matrix[j]
        high = value.astype(BF16)
        low = (value - high.astype(F32)).astype(BF16)
        both = dot(jnp.concatenate([high, low], 0), spread, (0, 0))
        out[0, 128 * j : 128 * j + 128, :] = both[:, :128]
        out[1, 128 * j : 128 * j + 128, :] = both[:, 128:]


def terms(own, visiting, coulomb, tab, total, first, fa, fb, fc, fd):
    table = lambda at, rows, cols=256: tab[at : at + rows, :cols]
    for j in range(TILES):
        a = own[j].astype(F32)
        a_re, a_im = a[:NG], a[NG:]
        parts = []
        for ref in visiting:
            b = ref[j].astype(F32)
            b_re, b_im = b[:NG], b[NG:]
            parts += [a_re * b_re + a_im * b_im, a_im * b_re - a_re * b_im]
        density = jnp.concatenate(parts, 0).astype(BF16)
        fa[128 * j : 128 * j + 128, :] = dot(density, table(0, 240), (0, 0)).astype(BF16)
    forward, inverse = table(480, 160, 160), table(640, 160, 160)
    for i in range(10):
        at = 160 * i
        a, b = fa[at : at + 80, :], fa[at + 80 : at + 160, :]
        field = jnp.concatenate(
            [jnp.concatenate([a[:, :128], b[:, :128]], 1), jnp.concatenate([a[:, 128:], b[:, 128:]], 1)], 0
        )
        r = dot(forward, field, (1, 0))
        for c in range(2):
            fb[c, at : at + 80, :] = r[80 * c : 80 * c + 80, :128]
            fb[c, at + 80 : at + 160, :] = r[80 * c : 80 * c + 80, 128:]
    for i in range(10):
        halves, scales = [], []
        for h in range(2):
            z = 4 * i + 2 * h
            halves.append(
                jnp.concatenate([fb[c, pl.ds(z + q, NG, stride=NG), :] for c in range(2) for q in range(2)], 0)
            )
            scales.append(jnp.concatenate([coulomb[pl.ds(z + q, NG, stride=NG), :] for q in range(2)] * 2, 0))
        field = jnp.concatenate(halves, 1).astype(BF16)
        r = dot(forward, field, (1, 0)).astype(BF16).astype(F32)
        scaled = (r * jnp.concatenate(scales, 1)).astype(BF16)
        r = dot(inverse, scaled, (1, 0))
        for h in range(2):
            for c in range(2):
                for q in range(2):
                    at = 80 * c + NG * q
                    fc[c, pl.ds(4 * i + 2 * h + q, NG, stride=NG), :] = r[at : at + NG, 128 * h : 128 * h + 128]
    for i in range(10):
        at = 160 * i
        field = jnp.concatenate(
            [jnp.concatenate([fc[c, at : at + 80, :], fc[c, at + 80 : at + 160, :]], 1) for c in range(2)], 0
        ).astype(BF16)
        r = dot(inverse, field, (1, 0)).astype(BF16)
        fd[at : at + 80, :] = jnp.concatenate([r[:80, :128], r[80:, :128]], 1)
        fd[at + 80 : at + 160, :] = jnp.concatenate([r[:80, 128:], r[80:, 128:]], 1)
    for j in range(TILES):
        wave = dot(table(240, 240), fd[128 * j : 128 * j + 128, :], (1, 1))
        re = im = 0.0
        for t, ref in enumerate(visiting):
            b = ref[j].astype(F32)
            b_re, b_im = b[:NG], b[NG:]
            w_re, w_im = wave[80 * t : 80 * t + NG], wave[80 * t + NG : 80 * t + 80]
            re = re + (b_re * w_re - b_im * w_im)
            im = im + (b_re * w_im + b_im * w_re)
        value = jnp.concatenate([re, im], 0)
        total[j] = value if first else (total[j] + value) * WEIGHT


def kernel(
    orbitals, coulomb, tables_ref, out,
    flat, kernel_flat, tab, matrix, kernel_matrix, odd, own, vis, passing, total, scale, fa, fb, fc, fd, out_flat,
    local_sem, send_sem, recv_sem,
):
    n, k = lax.axis_index("band"), lax.axis_index("kpt")
    core = lax.rem(n, 2)
    sibling = n + 1 - 2 * core
    behind, ahead = lax.rem(n + NBLOCK - 2, NBLOCK), lax.rem(n + 2, NBLOCK)
    k_behind, k_ahead = lax.rem(k + NK - 1, NK), lax.rem(k + 1, NK)
    k_beside, k_corner = lax.rem(k + 4, NK), lax.rem(k + 3, NK)
    turns, turned = lax.rem(k, 4) == 3, lax.rem(k, 4) == 0

    loads = [
        pltpu.make_async_copy(orbitals.at[0, 0], flat, local_sem.at[0]),
        pltpu.make_async_copy(coulomb.at[0], kernel_flat, local_sem.at[1]),
        pltpu.make_async_copy(tables_ref, tab, local_sem.at[2]),
    ]
    for load in loads:
        load.start()
    barrier = pltpu.get_barrier_semaphore()
    peers = [(behind, k), (n, k_behind), (sibling, k), (behind, k_behind), (n, k_corner), (n, k_beside), (behind, k_beside)]
    for peer in peers:
        pl.semaphore_signal(barrier, inc=1, device_id=peer, device_id_type=MESH)
    loads[0].wait()
    matrix_from_flat(flat, matrix, odd)
    own[...] = matrix[...].astype(BF16)
    pl.semaphore_wait(barrier, len(peers))

    used = [0]

    def copy(src, dst, peer, arrives=None):
        at = used[0]
        used[0] += 1
        arrives = at if arrives is None else arrives
        return pltpu.make_async_remote_copy(
            src_ref=src, dst_ref=dst, send_sem=send_sem.at[at], recv_sem=recv_sem.at[arrives],
            device_id=peer, device_id_type=MESH,
        )

    def chunk(ref, c):
        return ref.at[pl.ds(c[0], c[1])]

    to_ahead = [copy(chunk(own, c), chunk(vis.at[0], c), (ahead, k)) for c in CHUNKS]
    to_next_k = [copy(chunk(own, c), chunk(vis.at[2], c), (n, k_ahead), 18 + i) for i, c in enumerate(CHUNKS)]
    turn = copy(chunk(own, CHUNKS[0]), chunk(vis.at[3], CHUNKS[0]), (ahead, k_ahead), 20)
    round_y = copy(chunk(own, CHUNKS[1]), passing, (n, lax.rem(k + 5, NK)))
    pass_on = [
        copy(passing, chunk(vis.at[2], CHUNKS[1]), (n, k_beside), 19),
        copy(passing, chunk(vis.at[3], CHUNKS[1]), (ahead, k_beside), 21),
    ]
    on = [copy(chunk(vis.at[0], c), chunk(vis.at[3], c), (n, k_ahead), 20 + i) for i, c in enumerate(CHUNKS)]
    even_own = copy(own, vis.at[1], (sibling, k))
    even_partner = [copy(chunk(vis.at[2], c), chunk(vis.at[4], c), (sibling, k)) for c in CHUNKS]
    odd_own = [copy(chunk(vis.at[0], c), chunk(vis.at[1], c), (sibling, k)) for c in CHUNKS]
    odd_partner = [copy(chunk(vis.at[3], c), chunk(vis.at[4], c), (sibling, k)) for c in CHUNKS]

    def when(flag, *steps):
        @pl.when(flag)
        def _():
            for step in steps:
                step()

    straight, both = jnp.logical_not(turns), lambda copies, name: [getattr(c, name) for c in copies]
    when(turns, round_y.start, to_next_k[0].start, turn.start)
    for c in to_ahead:
        c.start()
    when(straight, *both(to_next_k, "start"))
    when(core == 0, even_own.start)
    loads[1].wait()
    matrix_from_flat(kernel_flat, kernel_matrix, odd)
    loads[2].wait()
    spread_coulomb(kernel_matrix, tab[800:960, :], scale)
    when(turned, round_y.wait_recv, *both(pass_on, "start"))
    for i in range(2):
        to_ahead[i].wait_recv()
        when(straight, on[i].start)
        when(core == 1, odd_own[i].start)

    def share_partner(flag):
        @pl.when(flag)
        def _():
            for i in range(2):
                to_next_k[i].wait_recv()
                when(core == 0, even_partner[i].start)

    share_partner(jnp.logical_not(turned))
    when(core == 0, *both(odd_own, "wait_recv"))
    when(core == 1, even_own.wait_recv)
    terms(own, [own, vis.at[1], vis.at[0]], scale.at[0], tab, total, True, fa, fb, fc, fd)
    share_partner(turned)
    for i in range(2):
        on[i].wait_recv()
        when(core == 1, odd_partner[i].start)
    when(core == 0, *both(odd_partner, "wait_recv"))
    when(core == 1, *both(even_partner, "wait_recv"))
    terms(own, [vis.at[2], vis.at[4], vis.at[3]], scale.at[1], tab, total, False, fa, fb, fc, fd)
    flat_from_matrix(total, out_flat, odd)
    store = pltpu.make_async_copy(out_flat, out.at[0, 0], local_sem.at[0])
    store.start()
    for c in to_ahead:
        c.wait_send()
    when(turns, round_y.wait_send, to_next_k[0].wait_send, turn.wait_send)
    when(straight, *both(to_next_k + on, "wait_send"))
    when(turned, *both(pass_on, "wait_send"))
    when(core == 0, even_own.wait_send, *both(even_partner, "wait_send"))
    when(core == 1, *both(odd_own + odd_partner, "wait_send"))
    store.wait()


def shards(orbitals, coulomb):
    field = (TILES, 2 * NG, 128)
    vmem = pltpu.VMEM
    return pl.pallas_call(
        kernel,
        out_shape=jax.ShapeDtypeStruct(orbitals.shape, F32),
        in_specs=[pl.BlockSpec(memory_space=pl.ANY)] * 3,
        out_specs=pl.BlockSpec(memory_space=pl.ANY),
        scratch_shapes=[
            vmem((2, 64000), BF16), vmem((2, 64000), F32), vmem((960, 256), BF16), vmem(field, F32), vmem(field, F32),
            vmem((14, 48, 128), F32), vmem(field, BF16), vmem((5, *field), BF16), vmem((6, 2 * NG, 128), BF16), vmem(field, F32), vmem((2, ROWS, 128), F32),
            vmem((ROWS, 256), BF16), vmem((2, 1600, 128), F32), vmem((2, 1600, 128), F32), vmem((ROWS, 256), BF16),
            vmem((2, 64000), F32), pltpu.SemaphoreType.DMA((3,)), pltpu.SemaphoreType.DMA((18,)), pltpu.SemaphoreType.DMA((22,)),
        ],
        compiler_params=pltpu.CompilerParams(collective_id=0, has_side_effects=True, vmem_limit_bytes=56 << 20),
    )(orbitals, coulomb, jnp.asarray(tables()))


def solution(mesh):
    return jax.shard_map(
        shards,
        mesh=mesh,
        in_specs=(P("kpt", "band", None, None), P("kpt", None, None)),
        out_specs=P("kpt", "band", None, None),
        check_vma=False,
    )
```

```python
import math

import jax
import jax.numpy as jnp
import ml_dtypes
import numpy as np
from jax import lax
from jax.experimental import pallas as pl
from jax.experimental.pallas import tpu as pltpu
from jax.sharding import PartitionSpec as P

NG = 40
KSTEPS = 2
BSTEPS = 2
TERMS = BSTEPS + 1
PAIR = 2
STEPS_OF = ((0, 1), (0, 0), (1, 1))
NBLOCK = 32
NK = 8
WEIGHT = -1.0 / (KSTEPS * TERMS)
BF16 = jnp.bfloat16
F32 = jnp.float32
MESH = pl.DeviceIdType.MESH
TILES = 13
ROWS = TILES * 128
CHUNKS = ((0, 7), (7, 6))


def tables():
    points = np.arange(NG)
    angle = (points[:, None] * points[None, :] % NG) * (2.0 * math.pi / NG)
    scale = 1.0 / math.sqrt(NG)
    c, s = (
        (f(angle) * scale).astype(ml_dtypes.bfloat16).astype(np.float32) for f in (np.cos, np.sin)
    )
    first = np.zeros((PAIR, 2, NG, 2, 128), np.float32)
    last = np.zeros((PAIR, 2, NG, 2, 128), np.float32)
    for t in range(PAIR):
        lanes = slice(NG * t, NG * t + NG)
        first[t, 0, :, 0, lanes] = c
        first[t, 1, :, 0, lanes] = s
        first[t, 0, :, 1, lanes] = -s
        first[t, 1, :, 1, lanes] = c
        last[t, 0, :, 0, lanes] = c
        last[t, 0, :, 1, lanes] = -s
        last[t, 1, :, 1, lanes] = c
        last[t, 1, :, 0, lanes] = s

    def rows(sign):
        table = np.zeros((2, 2, NG, 2, 2, NG), np.float32)
        for i in range(2):
            table[0, i, :, 0, i, :] = c
            table[0, i, :, 1, i, :] = sign * s
            table[1, i, :, 0, i, :] = -sign * s
            table[1, i, :, 1, i, :] = c
        return np.pad(table.reshape(160, 160), ((0, 0), (0, 96)))

    spread = np.zeros((2, 2, NG, 4, 128), np.float32)
    for group, steps in enumerate(STEPS_OF):
        for t, step in enumerate(steps):
            for half in range(2):
                spread[half, step, points, group, NG * t + points] = 1
    spread = spread.reshape(160, 512)
    parts = [first.reshape(160, 256), last.reshape(160, 256), rows(1.0), rows(-1.0), spread[:, :256], spread[:, 256:]]
    return np.concatenate(parts, 0).astype(ml_dtypes.bfloat16)


def matrix_from_flat(flat, matrix, odd):
    for a in range(NG // 2):
        for j in range(25):
            at = 128 * (25 * a + j)
            tile = flat[:, at : at + 128].astype(F32)
            if j <= 12:
                matrix[j, pl.ds(2 * a, 2, stride=NG), :] = tile
            if j >= 12:
                odd[j - 12, pl.ds(a, 2, stride=24), :] = tile
    lane = lax.broadcasted_iota(jnp.int32, (NG // 2, 128), 1)
    for c in range(2):
        here = pltpu.roll(odd[0, 24 * c : 24 * c + 20, :], 64, 1)
        for j in range(TILES):
            after = pltpu.roll(odd[j + 1, 24 * c : 24 * c + 20, :], 64, 1) if j < 12 else here
            matrix[j, pl.ds(NG * c + 1, 20, stride=2), :] = jnp.where(lane < 64, here, after)
            here = after


def flat_from_matrix(matrix, flat, odd):
    lane = lax.broadcasted_iota(jnp.int32, (NG // 2, 128), 1)
    for c in range(2):
        before = matrix[12, pl.ds(NG * c, 20, stride=2), :]
        for j in range(TILES):
            here = pltpu.roll(matrix[j, pl.ds(NG * c + 1, 20, stride=2), :], 64, 1)
            odd[j, 24 * c : 24 * c + 20, :] = jnp.where(lane < 64, before, here)
            before = here
    for a in range(NG // 2):
        for j in range(25):
            at = 128 * (25 * a + j)
            flat[:, at : at + 128] = (
                matrix[j, pl.ds(2 * a, 2, stride=NG), :] if j < 12 else odd[j - 12, pl.ds(a, 2, stride=24), :]
            )


def dot(a, b, on):
    return lax.dot_general(a, b, ((on[:1], on[1:]), ((), ())), preferred_element_type=F32)


def spread_coulomb(matrix, tab, out):
    for j in range(TILES):
        value = matrix[j]
        high = value.astype(BF16)
        low = (value - high.astype(F32)).astype(BF16)
        value = jnp.concatenate([high, low], 0)
        both = dot(value, tab[640:800, :], (0, 0))
        out[0, 128 * j : 128 * j + 128, :] = both[:, :128]
        out[1, 128 * j : 128 * j + 128, :] = both[:, 128:]
        out[2, 128 * j : 128 * j + 128, :] = dot(value, tab[800:960, :128], (0, 0))


def terms(block, visiting, coulomb, tab, total, last, fa, fb, fc, fd):
    table = lambda at, rows, cols=256: tab[at : at + rows, :cols]
    for j in range(TILES):
        a = block[j].astype(F32)
        a_re, a_im = a[:NG], a[NG:]
        parts = []
        for ref in visiting:
            b = ref[j].astype(F32)
            b_re, b_im = b[:NG], b[NG:]
            parts += [a_re * b_re + a_im * b_im, a_im * b_re - a_re * b_im]
        density = jnp.concatenate(parts, 0).astype(BF16)
        fa[128 * j : 128 * j + 128, :] = dot(density, table(0, 160), (0, 0)).astype(BF16)
    forward, inverse = table(320, 160, 160), table(480, 160, 160)
    for i in range(10):
        at = 160 * i
        a, b = fa[at : at + 80, :], fa[at + 80 : at + 160, :]
        field = jnp.concatenate(
            [jnp.concatenate([a[:, :128], b[:, :128]], 1), jnp.concatenate([a[:, 128:], b[:, 128:]], 1)], 0
        )
        r = dot(forward, field, (1, 0))
        for c in range(2):
            fb[c, at : at + 80, :] = r[80 * c : 80 * c + 80, :128]
            fb[c, at + 80 : at + 160, :] = r[80 * c : 80 * c + 80, 128:]
    for i in range(10):
        halves, scales = [], []
        for h in range(2):
            z = 4 * i + 2 * h
            halves.append(
                jnp.concatenate([fb[c, pl.ds(z + q, NG, stride=NG), :] for c in range(2) for q in range(2)], 0)
            )
            scales.append(jnp.concatenate([coulomb[pl.ds(z + q, NG, stride=NG), :] for q in range(2)] * 2, 0))
        field = jnp.concatenate(halves, 1).astype(BF16)
        r = dot(forward, field, (1, 0)).astype(BF16).astype(F32)
        scaled = (r * jnp.concatenate(scales, 1)).astype(BF16)
        r = dot(inverse, scaled, (1, 0))
        for h in range(2):
            for c in range(2):
                for q in range(2):
                    at = 80 * c + NG * q
                    fc[c, pl.ds(4 * i + 2 * h + q, NG, stride=NG), :] = r[at : at + NG, 128 * h : 128 * h + 128]
    for i in range(10):
        at = 160 * i
        field = jnp.concatenate(
            [jnp.concatenate([fc[c, at : at + 80, :], fc[c, at + 80 : at + 160, :]], 1) for c in range(2)], 0
        ).astype(BF16)
        r = dot(inverse, field, (1, 0)).astype(BF16)
        fd[at : at + 80, :] = jnp.concatenate([r[:80, :128], r[80:, :128]], 1)
        fd[at + 80 : at + 160, :] = jnp.concatenate([r[:80, 128:], r[80:, 128:]], 1)
    for j in range(TILES):
        wave = dot(table(160, 160), fd[128 * j : 128 * j + 128, :], (1, 1))
        re = im = 0.0
        for t, ref in enumerate(visiting):
            b = ref[j].astype(F32)
            b_re, b_im = b[:NG], b[NG:]
            w_re, w_im = wave[80 * t : 80 * t + NG], wave[80 * t + NG : 80 * t + 80]
            re = re + (b_re * w_re - b_im * w_im)
            im = im + (b_re * w_im + b_im * w_re)
        value = jnp.concatenate([re, im], 0)
        total[j] = (total[j] + value) * WEIGHT if last else total[j] + value


def kernel(
    orbitals, coulomb, tables_ref, out,
    flat, kernel_flat, tab, matrix, kernel_matrix, odd, vis, passing, total, scale, fa, fb, fc, fd, out_flat,
    local_sem, send_sem, recv_sem,
):
    n, k = lax.axis_index("band"), lax.axis_index("kpt")
    core = lax.rem(n, 2)
    sibling = n + 1 - 2 * core
    behind, ahead = lax.rem(n + NBLOCK - 2, NBLOCK), lax.rem(n + 2, NBLOCK)
    k_behind, k_ahead = lax.rem(k + NK - 1, NK), lax.rem(k + 1, NK)
    k_beside, k_corner = lax.rem(k + 4, NK), lax.rem(k + 3, NK)
    late, on_time, to_late = n < 2, n >= 2, n >= NBLOCK - 2
    turns, turned = lax.rem(k, 4) == 3, lax.rem(k, 4) == 0

    loads = [
        pltpu.make_async_copy(orbitals.at[0, 0], flat, local_sem.at[0]),
        pltpu.make_async_copy(coulomb.at[0], kernel_flat, local_sem.at[1]),
        pltpu.make_async_copy(tables_ref, tab, local_sem.at[2]),
    ]
    for load in loads:
        load.start()
    barrier = pltpu.get_barrier_semaphore()
    peers = [(behind, k), (n, k_behind), (sibling, k), (n, k_corner), (n, k_beside), (behind, k_beside)]
    for peer in peers:
        pl.semaphore_signal(barrier, inc=1, device_id=peer, device_id_type=MESH)
    loads[0].wait()
    matrix_from_flat(flat, matrix, odd)
    vis[0] = matrix[...].astype(BF16)
    pl.semaphore_wait(barrier, len(peers))

    used = [0]

    def copy(src, dst, peer, arrives=None):
        at = used[0]
        used[0] += 1
        arrives = at if arrives is None else arrives
        return pltpu.make_async_remote_copy(
            src_ref=src, dst_ref=dst, send_sem=send_sem.at[at], recv_sem=recv_sem.at[arrives],
            device_id=peer, device_id_type=MESH,
        )

    def chunk(ref, c):
        return ref.at[pl.ds(c[0], c[1])]

    def copies(src, dst, peer, arrives=None):
        arrives = (None, None) if arrives is None else (arrives, arrives + 1)
        return [copy(chunk(vis.at[src], c), chunk(vis.at[dst], c), peer, at) for c, at in zip(CHUNKS, arrives)]

    to_ahead = copies(0, 3, (ahead, k))
    to_next_k = copies(0, 1, (n, k_ahead), 24)
    on_x = copies(1, 5, (ahead, k), 26)
    on_y = copy(chunk(vis.at[3], CHUNKS[0]), chunk(vis.at[5], CHUNKS[0]), (n, k_ahead), 26)
    round_y = [copy(chunk(vis.at[0], c), chunk(passing, c), (n, lax.rem(k + 5, NK))) for c in CHUNKS]
    pass_on = [
        copy(chunk(passing, c), chunk(vis.at[dst], c), peer, at + i)
        for i, c in enumerate(CHUNKS)
        for dst, peer, at in ((1, (n, k_beside), 24), (5, (ahead, k_beside), 26))
    ]
    even_own, even_partner = copies(0, 2, (sibling, k)), copies(1, 4, (sibling, k))
    odd_own, odd_partner = copies(3, 2, (sibling, k)), copies(5, 4, (sibling, k))

    def when(flag, *steps):
        @pl.when(flag)
        def _():
            for step in steps:
                step()

    def both(copies, name):
        return [getattr(c, name) for c in copies]

    straight, inner = jnp.logical_not(turns), jnp.logical_not(turned)
    when(turns, round_y[0].start)
    for c in to_ahead:
        c.start()
    when(straight, *both(to_next_k, "start"))
    when(core == 0, *both(even_own, "start"))
    total[...] = jnp.zeros_like(total)
    loads[1].wait()
    matrix_from_flat(kernel_flat, kernel_matrix, odd)
    loads[2].wait()
    spread_coulomb(kernel_matrix, tab, scale)
    when(turns, round_y[0].wait_send, round_y[1].start)
    for i in range(2):
        when(turned, round_y[i].wait_recv, *both(pass_on[2 * i : 2 * i + 2], "start"))

    def partner(flag):
        @pl.when(flag)
        def _():
            for i in range(2):
                to_next_k[i].wait_recv()
                when(inner if i == 1 else inner & to_late, on_x[i].start)
                when(core == 0, even_partner[i].start)

    def block_behind(flag):
        @pl.when(flag)
        def _():
            for i in range(2):
                to_ahead[i].wait_recv()
                if i == 0:
                    when(straight & on_time, on_y.start)
                when(core == 1, odd_own[i].start)

    def from_sibling(flag):
        when(flag & (core == 0), *both(odd_own, "wait_recv"))
        when(flag & (core == 1), *both(even_own, "wait_recv"))

    def add(group, last=False):
        pair = [vis.at[2 * group], vis.at[2 * group + 1]]
        terms(vis.at[0], pair, scale.at[group], tab, total, last, fa, fb, fc, fd)

    swap, keep = turned & on_time, jnp.logical_not(turned & on_time)
    partner(inner)
    block_behind(on_time)
    partner(turned & late)
    from_sibling(swap)
    add(lax.select(swap, 1, 0))
    partner(swap)
    block_behind(late)
    from_sibling(keep)
    add(lax.select(swap, 0, 1))
    for i in range(2):
        on_x[i].wait_recv()
        when(core == 1, odd_partner[i].start)
    when(core == 0, *both(odd_partner, "wait_recv"))
    when(core == 1, *both(even_partner, "wait_recv"))
    add(2, True)
    flat_from_matrix(total, out_flat, odd)
    store = pltpu.make_async_copy(out_flat, out.at[0, 0], local_sem.at[0])
    store.start()
    for c in to_ahead:
        c.wait_send()
    when(turns, round_y[1].wait_send)
    when(straight, *both(to_next_k, "wait_send"))
    when(inner, on_x[1].wait_send)
    when(inner & to_late, on_x[0].wait_send)
    when(straight & on_time, on_y.wait_send)
    when(turned, *both(pass_on, "wait_send"))
    when(core == 0, *both(even_own + even_partner, "wait_send"))
    when(core == 1, *both(odd_own + odd_partner, "wait_send"))
    store.wait()


def shards(orbitals, coulomb):
    field = (TILES, 2 * NG, 128)
    vmem = pltpu.VMEM
    return pl.pallas_call(
        kernel,
        out_shape=jax.ShapeDtypeStruct(orbitals.shape, F32),
        in_specs=[pl.BlockSpec(memory_space=pl.ANY)] * 3,
        out_specs=pl.BlockSpec(memory_space=pl.ANY),
        scratch_shapes=[
            vmem((2, 64000), BF16), vmem((2, 64000), F32), vmem((960, 256), BF16), vmem(field, F32), vmem(field, F32),
            vmem((14, 48, 128), F32), vmem((6, *field), BF16), vmem(field, BF16), vmem(field, F32), vmem((3, ROWS, 128), F32),
            vmem((ROWS, 256), BF16), vmem((2, 1600, 128), F32), vmem((2, 1600, 128), F32), vmem((ROWS, 256), BF16),
            vmem((2, 64000), F32), pltpu.SemaphoreType.DMA((3,)), pltpu.SemaphoreType.DMA((24,)), pltpu.SemaphoreType.DMA((28,)),
        ],
        compiler_params=pltpu.CompilerParams(collective_id=0, has_side_effects=True, vmem_limit_bytes=56 << 20),
    )(orbitals, coulomb, jnp.asarray(tables()))


def solution(mesh):
    return jax.shard_map(
        shards,
        mesh=mesh,
        in_specs=(P("kpt", "band", None, None), P("kpt", None, None)),
        out_specs=P("kpt", "band", None, None),
        check_vma=False,
    )
```

```python
import math

import jax
import jax.numpy as jnp
import ml_dtypes
import numpy as np
from jax import lax
from jax.experimental import pallas as pl
from jax.experimental.pallas import tpu as pltpu
from jax.sharding import PartitionSpec as P

NG = 40
KSTEPS = 2
BSTEPS = 2
TERMS = BSTEPS + 1
PAIR = 2
STEPS_OF = ((0, 1), (0, 0), (1, 1))
NBLOCK = 32
NK = 8
WEIGHT = -1.0 / (KSTEPS * TERMS)
BF16 = jnp.bfloat16
F32 = jnp.float32
MESH = pl.DeviceIdType.MESH
TILES = 13
ROWS = TILES * 128
CHUNKS = ((0, 7), (7, 6))


def tables():
    points = np.arange(NG)
    angle = (points[:, None] * points[None, :] % NG) * (2.0 * math.pi / NG)
    scale = 1.0 / math.sqrt(NG)
    c, s = (
        (f(angle) * scale).astype(ml_dtypes.bfloat16).astype(np.float32) for f in (np.cos, np.sin)
    )
    first = np.zeros((PAIR, 2, NG, 2, 128), np.float32)
    last = np.zeros((PAIR, 2, NG, 2, 128), np.float32)
    for t in range(PAIR):
        lanes = slice(NG * t, NG * t + NG)
        first[t, 0, :, 0, lanes] = c
        first[t, 1, :, 0, lanes] = s
        first[t, 0, :, 1, lanes] = -s
        first[t, 1, :, 1, lanes] = c
        last[t, 0, :, 0, lanes] = c
        last[t, 0, :, 1, lanes] = -s
        last[t, 1, :, 1, lanes] = c
        last[t, 1, :, 0, lanes] = s

    def rows(sign):
        table = np.zeros((2, 2, NG, 2, 2, NG), np.float32)
        for i in range(2):
            table[0, i, :, 0, i, :] = c
            table[0, i, :, 1, i, :] = sign * s
            table[1, i, :, 0, i, :] = -sign * s
            table[1, i, :, 1, i, :] = c
        return np.pad(table.reshape(160, 160), ((0, 0), (0, 96)))

    spread = np.zeros((2, 2, NG, 4, 128), np.float32)
    for group, steps in enumerate(STEPS_OF):
        for t, step in enumerate(steps):
            for half in range(2):
                spread[half, step, points, group, NG * t + points] = 1
    spread = spread.reshape(160, 512)
    parts = [first.reshape(160, 256), last.reshape(160, 256), rows(1.0), rows(-1.0), spread[:, :256], spread[:, 256:]]
    return np.concatenate(parts, 0).astype(ml_dtypes.bfloat16)


def matrix_from_flat(flat, matrix, odd):
    for a in range(NG // 2):
        for j in range(25):
            at = 128 * (25 * a + j)
            tile = flat[:, at : at + 128].astype(F32)
            if j <= 12:
                matrix[j, pl.ds(2 * a, 2, stride=NG), :] = tile
            if j >= 12:
                odd[j - 12, pl.ds(a, 2, stride=24), :] = tile
    lane = lax.broadcasted_iota(jnp.int32, (NG // 2, 128), 1)
    for c in range(2):
        here = pltpu.roll(odd[0, 24 * c : 24 * c + 20, :], 64, 1)
        for j in range(TILES):
            after = pltpu.roll(odd[j + 1, 24 * c : 24 * c + 20, :], 64, 1) if j < 12 else here
            matrix[j, pl.ds(NG * c + 1, 20, stride=2), :] = jnp.where(lane < 64, here, after)
            here = after


def flat_from_matrix(matrix, flat, odd, done):
    lane = lax.broadcasted_iota(jnp.int32, (NG // 2, 128), 1)
    for c in range(2):
        before = matrix[12, pl.ds(NG * c, 20, stride=2), :]
        for j in range(TILES):
            here = pltpu.roll(matrix[j, pl.ds(NG * c + 1, 20, stride=2), :], 64, 1)
            odd[j, 24 * c : 24 * c + 20, :] = jnp.where(lane < 64, before, here)
            before = here
    for a in range(NG // 2):
        for j in range(25):
            at = 128 * (25 * a + j)
            flat[:, at : at + 128] = (
                matrix[j, pl.ds(2 * a, 2, stride=NG), :] if j < 12 else odd[j - 12, pl.ds(a, 2, stride=24), :]
            )
        done(a)


def dot(a, b, on):
    return lax.dot_general(a, b, ((on[:1], on[1:]), ((), ())), preferred_element_type=F32)


def spread_coulomb(matrix, tab, out):
    for j in range(TILES):
        value = matrix[j]
        high = value.astype(BF16)
        low = (value - high.astype(F32)).astype(BF16)
        value = jnp.concatenate([high, low], 0)
        both = dot(value, tab[640:800, :], (0, 0))
        out[0, 128 * j : 128 * j + 128, :] = both[:, :128]
        out[1, 128 * j : 128 * j + 128, :] = both[:, 128:]
        out[2, 128 * j : 128 * j + 128, :] = dot(value, tab[800:960, :128], (0, 0))


def terms(block, visiting, coulomb, tab, total, last, fa, fb, fc, fd):
    table = lambda at, rows, cols=256: tab[at : at + rows, :cols]
    for j in range(TILES):
        a = block[j].astype(F32)
        a_re, a_im = a[:NG], a[NG:]
        parts = []
        for ref in visiting:
            b = ref[j].astype(F32)
            b_re, b_im = b[:NG], b[NG:]
            parts += [a_re * b_re + a_im * b_im, a_im * b_re - a_re * b_im]
        density = jnp.concatenate(parts, 0).astype(BF16)
        fa[128 * j : 128 * j + 128, :] = dot(density, table(0, 160), (0, 0)).astype(BF16)
    forward, inverse = table(320, 160, 160), table(480, 160, 160)
    for i in range(10):
        at = 160 * i
        a, b = fa[at : at + 80, :], fa[at + 80 : at + 160, :]
        field = jnp.concatenate(
            [jnp.concatenate([a[:, :128], b[:, :128]], 1), jnp.concatenate([a[:, 128:], b[:, 128:]], 1)], 0
        )
        r = dot(forward, field, (1, 0))
        for c in range(2):
            fb[c, at : at + 80, :] = r[80 * c : 80 * c + 80, :128]
            fb[c, at + 80 : at + 160, :] = r[80 * c : 80 * c + 80, 128:]
    for i in range(10):
        halves, scales = [], []
        for h in range(2):
            z = 4 * i + 2 * h
            halves.append(
                jnp.concatenate([fb[c, pl.ds(z + q, NG, stride=NG), :] for c in range(2) for q in range(2)], 0)
            )
            scales.append(jnp.concatenate([coulomb[pl.ds(z + q, NG, stride=NG), :] for q in range(2)] * 2, 0))
        field = jnp.concatenate(halves, 1).astype(BF16)
        r = dot(forward, field, (1, 0)).astype(BF16).astype(F32)
        scaled = (r * jnp.concatenate(scales, 1)).astype(BF16)
        r = dot(inverse, scaled, (1, 0))
        for h in range(2):
            for c in range(2):
                for q in range(2):
                    at = 80 * c + NG * q
                    fc[c, pl.ds(4 * i + 2 * h + q, NG, stride=NG), :] = r[at : at + NG, 128 * h : 128 * h + 128]
    for i in range(10):
        at = 160 * i
        field = jnp.concatenate(
            [jnp.concatenate([fc[c, at : at + 80, :], fc[c, at + 80 : at + 160, :]], 1) for c in range(2)], 0
        ).astype(BF16)
        r = dot(inverse, field, (1, 0)).astype(BF16)
        fd[at : at + 80, :] = jnp.concatenate([r[:80, :128], r[80:, :128]], 1)
        fd[at + 80 : at + 160, :] = jnp.concatenate([r[:80, 128:], r[80:, 128:]], 1)
    for j in range(TILES):
        wave = dot(table(160, 160), fd[128 * j : 128 * j + 128, :], (1, 1))
        re = im = 0.0
        for t, ref in enumerate(visiting):
            b = ref[j].astype(F32)
            b_re, b_im = b[:NG], b[NG:]
            w_re, w_im = wave[80 * t : 80 * t + NG], wave[80 * t + NG : 80 * t + 80]
            re = re + (b_re * w_re - b_im * w_im)
            im = im + (b_re * w_im + b_im * w_re)
        value = jnp.concatenate([re, im], 0)
        total[j] = (total[j] + value) * WEIGHT if last else total[j] + value


def kernel(
    orbitals, coulomb, tables_ref, total,
    flat, kernel_flat, tab, matrix, kernel_matrix, odd, vis, passing, scale, fa, fb, fc, fd,
    local_sem, send_sem, recv_sem,
):
    n, k = lax.axis_index("band"), lax.axis_index("kpt")
    core = lax.rem(n, 2)
    sibling = n + 1 - 2 * core
    behind, ahead = lax.rem(n + NBLOCK - 2, NBLOCK), lax.rem(n + 2, NBLOCK)
    k_behind, k_ahead = lax.rem(k + NK - 1, NK), lax.rem(k + 1, NK)
    k_beside, k_corner = lax.rem(k + 4, NK), lax.rem(k + 3, NK)
    late, on_time = n < 2, n >= 2
    turns, turned = lax.rem(k, 4) == 3, lax.rem(k, 4) == 0

    loads = [
        pltpu.make_async_copy(orbitals.at[0, 0], flat, local_sem.at[0]),
        pltpu.make_async_copy(coulomb.at[0], kernel_flat, local_sem.at[1]),
        pltpu.make_async_copy(tables_ref, tab, local_sem.at[2]),
    ]
    for load in loads:
        load.start()
    barrier = pltpu.get_barrier_semaphore()
    peers = [(behind, k), (n, k_behind), (sibling, k), (n, k_corner), (n, k_beside), (behind, k_beside)]
    for peer in peers:
        pl.semaphore_signal(barrier, inc=1, device_id=peer, device_id_type=MESH)
    loads[0].wait()
    matrix_from_flat(flat, matrix, odd)
    vis[0] = matrix[...].astype(BF16)
    pl.semaphore_wait(barrier, len(peers))

    used = [0]

    def copy(src, dst, peer, arrives=None):
        at = used[0]
        used[0] += 1
        arrives = at if arrives is None else arrives
        return pltpu.make_async_remote_copy(
            src_ref=src, dst_ref=dst, send_sem=send_sem.at[at], recv_sem=recv_sem.at[arrives],
            device_id=peer, device_id_type=MESH,
        )

    def chunk(ref, c):
        return ref.at[pl.ds(c[0], c[1])]

    def copies(src, dst, peer, arrives=None):
        arrives = (None, None) if arrives is None else (arrives, arrives + 1)
        return [copy(chunk(vis.at[src], c), chunk(vis.at[dst], c), peer, at) for c, at in zip(CHUNKS, arrives)]

    to_ahead = copies(0, 3, (ahead, k))
    to_next_k = copies(0, 1, (n, k_ahead), 24)
    on_x = copy(chunk(vis.at[1], CHUNKS[1]), chunk(vis.at[5], CHUNKS[1]), (ahead, k), 27)
    on_y = copy(chunk(vis.at[3], CHUNKS[0]), chunk(vis.at[5], CHUNKS[0]), (n, k_ahead), 26)
    round_y = [copy(chunk(vis.at[0], c), chunk(passing, c), (n, lax.rem(k + 5, NK))) for c in CHUNKS]
    pass_on = [
        copy(chunk(passing, c), chunk(vis.at[dst], c), peer, at + i)
        for i, c in enumerate(CHUNKS)
        for dst, peer, at in ((1, (n, k_beside), 24), (5, (ahead, k_beside), 26))
    ]
    even_own, even_partner = copies(0, 2, (sibling, k)), copies(1, 4, (sibling, k))
    odd_own, odd_partner = copies(3, 2, (sibling, k)), copies(5, 4, (sibling, k))

    def when(flag, *steps):
        @pl.when(flag)
        def _():
            for step in steps:
                step()

    def both(copies, name):
        return [getattr(c, name) for c in copies]

    straight, inner = jnp.logical_not(turns), jnp.logical_not(turned)
    when(turns, round_y[0].start)
    to_ahead[0].start()
    when(straight, to_next_k[1].start)
    when(core == 0, *both(even_own, "start"))
    total[...] = jnp.zeros_like(total)
    loads[1].wait()
    matrix_from_flat(kernel_flat, kernel_matrix, odd)
    loads[2].wait()
    spread_coulomb(kernel_matrix, tab, scale)
    when(turns, round_y[0].wait_send, round_y[1].start)
    when(straight, to_next_k[1].wait_send, to_next_k[0].start)
    to_ahead[0].wait_send()
    to_ahead[1].start()
    for i in range(2):
        when(turned, round_y[i].wait_recv, *both(pass_on[2 * i : 2 * i + 2], "start"))

    def partner(i, flag):
        @pl.when(flag)
        def _():
            to_next_k[i].wait_recv()
            if i == 1:
                when(inner, on_x.start)
            when(core == 0, even_partner[i].start)

    def block_behind(i, flag):
        @pl.when(flag)
        def _():
            to_ahead[i].wait_recv()
            if i == 0:
                when(straight, on_y.start)
            when(core == 1, odd_own[i].start)

    def from_sibling(flag):
        when(flag & (core == 0), *both(odd_own, "wait_recv"))
        when(flag & (core == 1), *both(even_own, "wait_recv"))

    def add(group, last=False):
        pair = [vis.at[2 * group], vis.at[2 * group + 1]]
        terms(vis.at[0], pair, scale.at[group], tab, total, last, fa, fb, fc, fd)

    swap, keep = turned & on_time, jnp.logical_not(turned & on_time)
    partner(1, inner)
    block_behind(0, on_time)
    partner(0, inner)
    block_behind(1, on_time)
    partner(0, turned & late)
    partner(1, turned & late)
    from_sibling(swap)
    add(lax.select(swap, 1, 0))
    partner(0, swap)
    partner(1, swap)
    block_behind(0, late)
    block_behind(1, late)
    from_sibling(keep)
    add(lax.select(swap, 0, 1))
    for i, arrived in enumerate((on_y, on_x)):
        arrived.wait_recv()
        when(core == 1, odd_partner[i].start)
    when(core == 0, *both(odd_partner, "wait_recv"))
    when(core == 1, *both(even_partner, "wait_recv"))
    add(2, True)
    to_ahead[1].wait_send()
    when(turns, round_y[1].wait_send)
    when(straight, to_next_k[0].wait_send, on_y.wait_send)
    when(inner, on_x.wait_send)
    when(turned, *both(pass_on, "wait_send"))
    when(core == 0, *both(even_own + even_partner, "wait_send"))
    when(core == 1, *both(odd_own + odd_partner, "wait_send"))


def write(total, out, odd, flat, sem):
    stores = [
        pltpu.make_async_copy(flat.at[:, pl.ds(at, 16000)], out.at[0, 0, :, pl.ds(at, 16000)], sem.at[i])
        for i, at in enumerate(range(0, 64000, 16000))
    ]

    def done(a):
        if a % 5 == 4:
            stores[a // 5].start()

    flat_from_matrix(total, flat, odd, done)
    for store in stores:
        store.wait()


def shards(orbitals, coulomb):
    field = (TILES, 2 * NG, 128)
    vmem = pltpu.VMEM
    total = pl.pallas_call(
        kernel,
        out_shape=pltpu.VMEM(field, F32),
        in_specs=[pl.BlockSpec(memory_space=pl.ANY)] * 3,
        out_specs=pl.BlockSpec(memory_space=pltpu.VMEM),
        scratch_shapes=[
            vmem((2, 64000), BF16), vmem((2, 64000), F32), vmem((960, 256), BF16), vmem(field, F32), vmem(field, F32),
            vmem((14, 48, 128), F32), vmem((6, *field), BF16), vmem(field, BF16), vmem((3, ROWS, 128), F32),
            vmem((ROWS, 256), BF16), vmem((2, 1600, 128), F32), vmem((2, 1600, 128), F32), vmem((ROWS, 256), BF16),
            pltpu.SemaphoreType.DMA((3,)), pltpu.SemaphoreType.DMA((24,)), pltpu.SemaphoreType.DMA((28,)),
        ],
        compiler_params=pltpu.CompilerParams(collective_id=0, has_side_effects=True, vmem_limit_bytes=56 << 20),
    )(orbitals, coulomb, jnp.asarray(tables()))
    return pl.pallas_call(
        write,
        out_shape=jax.ShapeDtypeStruct(orbitals.shape, F32),
        in_specs=[pl.BlockSpec(memory_space=pltpu.VMEM)],
        out_specs=pl.BlockSpec(memory_space=pl.ANY),
        scratch_shapes=[vmem((14, 48, 128), F32), vmem((2, 64000), F32), pltpu.SemaphoreType.DMA((4,))],
        compiler_params=pltpu.CompilerParams(vmem_limit_bytes=16 << 20),
    )(total)


def solution(mesh):
    return jax.shard_map(
        shards,
        mesh=mesh,
        in_specs=(P("kpt", "band", None, None), P("kpt", None, None)),
        out_specs=P("kpt", "band", None, None),
        check_vma=False,
    )
```

```python
import math

import jax
import jax.numpy as jnp
import ml_dtypes
import numpy as np
from jax import lax
from jax.experimental import pallas as pl
from jax.experimental.pallas import tpu as pltpu
from jax.sharding import PartitionSpec as P

NG = 40
KSTEPS = 2
BSTEPS = 2
TERMS = BSTEPS + 1
STEPS_OF = ((0, 0, 0), (1, 1, 1), (0, 1, 1))
NBLOCK = 32
NK = 8
WEIGHT = -1.0 / (KSTEPS * TERMS)
BF16 = jnp.bfloat16
F32 = jnp.float32
MESH = pl.DeviceIdType.MESH
TILES = 13
ROWS = TILES * 128
CHUNKS = ((0, 7), (7, 6))


def tables():
    points = np.arange(NG)
    angle = (points[:, None] * points[None, :] % NG) * (2.0 * math.pi / NG)
    scale = 1.0 / math.sqrt(NG)
    c, s = (
        (f(angle) * scale).astype(ml_dtypes.bfloat16).astype(np.float32) for f in (np.cos, np.sin)
    )
    first = np.zeros((TERMS, 2, NG, 2, 128), np.float32)
    last = np.zeros((TERMS, 2, NG, 2, 128), np.float32)
    for t in range(TERMS):
        lanes = slice(NG * t, NG * t + NG)
        first[t, 0, :, 0, lanes] = c
        first[t, 1, :, 0, lanes] = s
        first[t, 0, :, 1, lanes] = -s
        first[t, 1, :, 1, lanes] = c
        last[t, 0, :, 0, lanes] = c
        last[t, 0, :, 1, lanes] = -s
        last[t, 1, :, 1, lanes] = c
        last[t, 1, :, 0, lanes] = s

    def rows(sign):
        table = np.zeros((2, 2, NG, 2, 2, NG), np.float32)
        for i in range(2):
            table[0, i, :, 0, i, :] = c
            table[0, i, :, 1, i, :] = sign * s
            table[1, i, :, 0, i, :] = -sign * s
            table[1, i, :, 1, i, :] = c
        return np.pad(table.reshape(160, 160), ((0, 0), (0, 96)))

    spread = np.zeros((2, 2, NG, 4, 128), np.float32)
    for group, steps in enumerate(STEPS_OF):
        for t, step in enumerate(steps):
            for half in range(2):
                spread[half, step, points, group, NG * t + points] = 1
    spread = spread.reshape(160, 512)
    parts = [first.reshape(240, 256), last.reshape(240, 256), rows(1.0), rows(-1.0), spread[:, :256], spread[:, 256:]]
    return np.concatenate(parts, 0).astype(ml_dtypes.bfloat16)


def matrix_from_flat(flat, matrix, odd):
    for a in range(NG // 2):
        for j in range(25):
            at = 128 * (25 * a + j)
            tile = flat[:, at : at + 128].astype(F32)
            if j <= 12:
                matrix[j, pl.ds(2 * a, 2, stride=NG), :] = tile
            if j >= 12:
                odd[j - 12, pl.ds(a, 2, stride=24), :] = tile
    lane = lax.broadcasted_iota(jnp.int32, (NG // 2, 128), 1)
    for c in range(2):
        here = pltpu.roll(odd[0, 24 * c : 24 * c + 20, :], 64, 1)
        for j in range(TILES):
            after = pltpu.roll(odd[j + 1, 24 * c : 24 * c + 20, :], 64, 1) if j < 12 else here
            matrix[j, pl.ds(NG * c + 1, 20, stride=2), :] = jnp.where(lane < 64, here, after)
            here = after


def flat_from_matrix(matrix, flat, odd, done):
    lane = lax.broadcasted_iota(jnp.int32, (NG // 2, 128), 1)
    for c in range(2):
        before = matrix[12, pl.ds(NG * c, 20, stride=2), :]
        for j in range(TILES):
            here = pltpu.roll(matrix[j, pl.ds(NG * c + 1, 20, stride=2), :], 64, 1)
            odd[j, 24 * c : 24 * c + 20, :] = jnp.where(lane < 64, before, here)
            before = here
    for a in range(NG // 2):
        for j in range(25):
            at = 128 * (25 * a + j)
            flat[:, at : at + 128] = (
                matrix[j, pl.ds(2 * a, 2, stride=NG), :] if j < 12 else odd[j - 12, pl.ds(a, 2, stride=24), :]
            )
        done(a)


def dot(a, b, on):
    return lax.dot_general(a, b, ((on[:1], on[1:]), ((), ())), preferred_element_type=F32)


def spread_coulomb(matrix, tab, out):
    for j in range(TILES):
        value = matrix[j]
        high = value.astype(BF16)
        low = (value - high.astype(F32)).astype(BF16)
        value = jnp.concatenate([high, low], 0)
        both = dot(value, tab[800:960, :], (0, 0))
        out[0, 128 * j : 128 * j + 128, :] = both[:, :128]
        out[1, 128 * j : 128 * j + 128, :] = both[:, 128:]
        out[2, 128 * j : 128 * j + 128, :] = dot(value, tab[960:1120, :128], (0, 0))


def terms(block, visiting, coulomb, tab, total, last, fa, fb, fc, fd):
    table = lambda at, rows, cols=256: tab[at : at + rows, :cols]
    rows = 2 * NG * len(visiting)
    for j in range(TILES):
        a = block[j].astype(F32)
        a_re, a_im = a[:NG], a[NG:]
        parts = []
        for ref in visiting:
            b = ref[j].astype(F32)
            b_re, b_im = b[:NG], b[NG:]
            parts += [a_re * b_re + a_im * b_im, a_im * b_re - a_re * b_im]
        density = jnp.concatenate(parts, 0).astype(BF16)
        fa[128 * j : 128 * j + 128, :] = dot(density, table(0, rows), (0, 0)).astype(BF16)
    forward, inverse = table(480, 160, 160), table(640, 160, 160)
    for i in range(10):
        at = 160 * i
        a, b = fa[at : at + 80, :], fa[at + 80 : at + 160, :]
        field = jnp.concatenate(
            [jnp.concatenate([a[:, :128], b[:, :128]], 1), jnp.concatenate([a[:, 128:], b[:, 128:]], 1)], 0
        )
        r = dot(forward, field, (1, 0))
        for c in range(2):
            fb[c, at : at + 80, :] = r[80 * c : 80 * c + 80, :128]
            fb[c, at + 80 : at + 160, :] = r[80 * c : 80 * c + 80, 128:]
    for i in range(10):
        halves, scales = [], []
        for h in range(2):
            z = 4 * i + 2 * h
            halves.append(
                jnp.concatenate([fb[c, pl.ds(z + q, NG, stride=NG), :] for c in range(2) for q in range(2)], 0)
            )
            scales.append(jnp.concatenate([coulomb[pl.ds(z + q, NG, stride=NG), :] for q in range(2)] * 2, 0))
        field = jnp.concatenate(halves, 1).astype(BF16)
        r = dot(forward, field, (1, 0)).astype(BF16).astype(F32)
        scaled = (r * jnp.concatenate(scales, 1)).astype(BF16)
        r = dot(inverse, scaled, (1, 0))
        for h in range(2):
            for c in range(2):
                for q in range(2):
                    at = 80 * c + NG * q
                    fc[c, pl.ds(4 * i + 2 * h + q, NG, stride=NG), :] = r[at : at + NG, 128 * h : 128 * h + 128]
    for i in range(10):
        at = 160 * i
        field = jnp.concatenate(
            [jnp.concatenate([fc[c, at : at + 80, :], fc[c, at + 80 : at + 160, :]], 1) for c in range(2)], 0
        ).astype(BF16)
        r = dot(inverse, field, (1, 0)).astype(BF16)
        fd[at : at + 80, :] = jnp.concatenate([r[:80, :128], r[80:, :128]], 1)
        fd[at + 80 : at + 160, :] = jnp.concatenate([r[:80, 128:], r[80:, 128:]], 1)
    for j in range(TILES):
        wave = dot(table(240, rows), fd[128 * j : 128 * j + 128, :], (1, 1))
        re = im = 0.0
        for t, ref in enumerate(visiting):
            b = ref[j].astype(F32)
            b_re, b_im = b[:NG], b[NG:]
            w_re, w_im = wave[80 * t : 80 * t + NG], wave[80 * t + NG : 80 * t + 80]
            re = re + (b_re * w_re - b_im * w_im)
            im = im + (b_re * w_im + b_im * w_re)
        value = jnp.concatenate([re, im], 0)
        total[j] = (total[j] + value) * WEIGHT if last else total[j] + value


def kernel(
    orbitals, coulomb, tables_ref, total,
    flat, kernel_flat, tab, matrix, kernel_matrix, odd, vis, passing, scale, fa, fb, fc, fd,
    local_sem, send_sem, recv_sem,
):
    n, k = lax.axis_index("band"), lax.axis_index("kpt")
    core = lax.rem(n, 2)
    sibling = n + 1 - 2 * core
    behind, ahead = lax.rem(n + NBLOCK - 2, NBLOCK), lax.rem(n + 2, NBLOCK)
    k_behind, k_ahead = lax.rem(k + NK - 1, NK), lax.rem(k + 1, NK)
    k_beside, k_corner = lax.rem(k + 4, NK), lax.rem(k + 3, NK)
    late, on_time = n < 2, n >= 2
    turns, turned = lax.rem(k, 4) == 3, lax.rem(k, 4) == 0

    barrier = pltpu.get_barrier_semaphore()

    def ready(*peers):
        for peer in peers:
            pl.semaphore_signal(barrier, inc=1, device_id=peer, device_id_type=MESH)

    ready((behind, k), (sibling, k))
    pl.when(jnp.logical_not(turned))(lambda: ready((n, k_behind)))
    pl.when(turned)(lambda: ready((n, k_corner), (n, k_beside), (behind, k_beside)))
    loads = [
        pltpu.make_async_copy(orbitals.at[0, 0], flat, local_sem.at[0]),
        pltpu.make_async_copy(coulomb.at[0], kernel_flat, local_sem.at[1]),
        pltpu.make_async_copy(tables_ref, tab, local_sem.at[2]),
    ]
    for load in loads:
        load.start()
    loads[0].wait()
    matrix_from_flat(flat, matrix, odd)
    vis[0] = matrix[:TILES].astype(BF16)
    pl.semaphore_wait(barrier, 3 + 2 * turned.astype(jnp.int32))

    used = [0]

    def copy(src, dst, peer, arrives=None):
        at = used[0]
        used[0] += 1
        arrives = at if arrives is None else arrives
        return pltpu.make_async_remote_copy(
            src_ref=src, dst_ref=dst, send_sem=send_sem.at[at], recv_sem=recv_sem.at[arrives],
            device_id=peer, device_id_type=MESH,
        )

    def chunk(ref, c):
        return ref.at[pl.ds(c[0], c[1])]

    def copies(src, dst, peer, arrives=None):
        arrives = (None, None) if arrives is None else (arrives, arrives + 1)
        return [copy(chunk(vis.at[src], c), chunk(vis.at[dst], c), peer, at) for c, at in zip(CHUNKS, arrives)]

    to_ahead = copies(0, 3, (ahead, k))
    to_next_k = copies(0, 1, (n, k_ahead), 24)
    on_x = copy(chunk(vis.at[1], CHUNKS[1]), chunk(vis.at[5], CHUNKS[1]), (ahead, k), 27)
    on_y = copy(chunk(vis.at[3], CHUNKS[0]), chunk(vis.at[5], CHUNKS[0]), (n, k_ahead), 26)
    round_y = [copy(chunk(vis.at[0], c), chunk(passing, c), (n, lax.rem(k + 5, NK))) for c in CHUNKS]
    pass_on = [
        copy(chunk(passing, c), chunk(vis.at[dst], c), peer, at + i)
        for i, c in enumerate(CHUNKS)
        for dst, peer, at in ((1, (n, k_beside), 24), (5, (ahead, k_beside), 26))
    ]
    even_own, even_partner = copies(0, 2, (sibling, k)), copies(1, 4, (sibling, k))
    odd_own, odd_partner = copies(3, 2, (sibling, k)), copies(5, 4, (sibling, k))

    def when(flag, *steps):
        @pl.when(flag)
        def _():
            for step in steps:
                step()

    def both(copies, name):
        return [getattr(c, name) for c in copies]

    straight, inner = jnp.logical_not(turns), jnp.logical_not(turned)
    when(turns, round_y[0].start)
    to_ahead[0].start()
    at_once = n >= NBLOCK - 2
    when(at_once, to_ahead[1].start)
    when(straight, to_next_k[1].start)
    when(core == 0, *both(even_own, "start"))
    total[:TILES] = jnp.zeros((TILES, 2 * NG, 128), F32)
    loads[1].wait()
    matrix_from_flat(kernel_flat, kernel_matrix, odd)
    loads[2].wait()
    spread_coulomb(kernel_matrix, tab, scale)
    when(turns, round_y[0].wait_send, round_y[1].start)
    when(straight, to_next_k[1].wait_send, to_next_k[0].start)
    when(jnp.logical_not(at_once), to_ahead[0].wait_send, to_ahead[1].start)
    @pl.when(turned)
    def _():
        terms(vis.at[0], [vis.at[0]], scale.at[0], tab, total, False, fa, fb, fc, fd)

    for i in range(2):
        when(turned, round_y[i].wait_recv, pass_on[2 * i + 1].start, pass_on[2 * i].start)

    def partner(i, flag):
        @pl.when(flag)
        def _():
            to_next_k[i].wait_recv()
            if i == 1:
                when(inner, on_x.start)
            when(core == 0, even_partner[i].start)

    def block_behind(i, flag):
        @pl.when(flag)
        def _():
            to_ahead[i].wait_recv()
            if i == 0:
                when(straight, on_y.start)
            when(core == 1, odd_own[i].start)

    early = turned | on_time

    def add(slots, steps, flag=None, last=False):
        def work():
            terms(vis.at[0], [vis.at[i] for i in slots], scale.at[steps], tab, total, last, fa, fb, fc, fd)

        work() if flag is None else pl.when(flag)(work)

    partner(1, inner)
    block_behind(0, early)
    partner(0, inner)
    block_behind(1, early)
    add((0, 1), 2, inner)
    block_behind(0, inner & late)
    block_behind(1, inner & late)
    when(core == 0, *both(odd_own, "wait_recv"))
    when(core == 1, *both(even_own, "wait_recv"))
    add((2, 3), 0)
    partner(0, turned)
    partner(1, turned)
    for i, arrived in enumerate((on_y, on_x)):
        arrived.wait_recv()
        when(core == 1, odd_partner[i].start)
    when(core == 0, *both(odd_partner, "wait_recv"))
    when(core == 1, *both(even_partner, "wait_recv"))
    add((4, 5), 1, inner, True)
    add((1, 4, 5), 1, turned, True)
    when(at_once, to_ahead[0].wait_send)
    to_ahead[1].wait_send()
    when(turns, round_y[1].wait_send)
    when(straight, to_next_k[0].wait_send, on_y.wait_send)
    when(inner, on_x.wait_send)
    when(turned, *both(pass_on, "wait_send"))
    when(core == 0, *both(even_own + even_partner, "wait_send"))
    when(core == 1, *both(odd_own + odd_partner, "wait_send"))


def write(total, out, odd, flat, sem):
    stores = [
        pltpu.make_async_copy(flat.at[:, pl.ds(at, 16000)], out.at[0, 0, :, pl.ds(at, 16000)], sem.at[i])
        for i, at in enumerate(range(0, 64000, 16000))
    ]

    def done(a):
        if a % 5 == 4:
            stores[a // 5].start()

    flat_from_matrix(total, flat, odd, done)
    for store in stores:
        store.wait()


def shards(orbitals, coulomb):
    field, spare = (TILES, 2 * NG, 128), (TILES + 4, 2 * NG, 128)
    vmem = pltpu.VMEM
    total = pl.pallas_call(
        kernel,
        out_shape=pltpu.VMEM(spare, F32),
        in_specs=[pl.BlockSpec(memory_space=pl.ANY)] * 3,
        out_specs=pl.BlockSpec(memory_space=pltpu.VMEM),
        scratch_shapes=[
            vmem((2, 64000), BF16), vmem((2, 64000), F32), vmem((1120, 256), BF16), vmem(spare, F32), vmem(spare, F32),
            vmem((TILES + 4, 48, 128), F32), vmem((6, *field), BF16), vmem(field, BF16), vmem((3, ROWS, 128), F32),
            vmem((ROWS, 256), BF16), vmem((2, 1600, 128), F32), vmem((2, 1600, 128), F32), vmem((ROWS, 256), BF16),
            pltpu.SemaphoreType.DMA((3,)), pltpu.SemaphoreType.DMA((24,)), pltpu.SemaphoreType.DMA((28,)),
        ],
        compiler_params=pltpu.CompilerParams(collective_id=0, has_side_effects=True, vmem_limit_bytes=56 << 20),
    )(orbitals, coulomb, jnp.asarray(tables()))
    return pl.pallas_call(
        write,
        out_shape=jax.ShapeDtypeStruct(orbitals.shape, F32),
        in_specs=[pl.BlockSpec(memory_space=pltpu.VMEM)],
        out_specs=pl.BlockSpec(memory_space=pl.ANY),
        scratch_shapes=[vmem((TILES + 4, 48, 128), F32), vmem((2, 64000), F32), pltpu.SemaphoreType.DMA((4,))],
        compiler_params=pltpu.CompilerParams(vmem_limit_bytes=16 << 20),
    )(total)


def solution(mesh):
    return jax.shard_map(
        shards,
        mesh=mesh,
        in_specs=(P("kpt", "band", None, None), P("kpt", None, None)),
        out_specs=P("kpt", "band", None, None),
        check_vma=False,
    )
```

```python
import math

import jax
import jax.numpy as jnp
import ml_dtypes
import numpy as np
from jax import lax
from jax.experimental import pallas as pl
from jax.experimental.pallas import tpu as pltpu
from jax.sharding import PartitionSpec as P

NG = 40
KSTEPS = 2
BSTEPS = 2
TERMS = BSTEPS + 1
STEPS_OF = ((0, 0, 0), (1, 1, 1), (0, 1, 1))
NBLOCK = 32
NK = 8
WEIGHT = -1.0 / (KSTEPS * TERMS)
BF16 = jnp.bfloat16
F32 = jnp.float32
MESH = pl.DeviceIdType.MESH
TILES = 13
ROWS = TILES * 128
CHUNKS = ((0, 5), (5, 8))


def tables():
    points = np.arange(NG)
    angle = (points[:, None] * points[None, :] % NG) * (2.0 * math.pi / NG)
    scale = 1.0 / math.sqrt(NG)
    c, s = (
        (f(angle) * scale).astype(ml_dtypes.bfloat16).astype(np.float32) for f in (np.cos, np.sin)
    )
    first = np.zeros((TERMS, 2, NG, 2, 128), np.float32)
    last = np.zeros((TERMS, 2, NG, 2, 128), np.float32)
    for t in range(TERMS):
        lanes = slice(NG * t, NG * t + NG)
        first[t, 0, :, 0, lanes] = c
        first[t, 1, :, 0, lanes] = s
        first[t, 0, :, 1, lanes] = -s
        first[t, 1, :, 1, lanes] = c
        last[t, 0, :, 0, lanes] = c
        last[t, 0, :, 1, lanes] = -s
        last[t, 1, :, 1, lanes] = c
        last[t, 1, :, 0, lanes] = s

    def rows(sign):
        table = np.zeros((2, 2, NG, 2, 2, NG), np.float32)
        for i in range(2):
            table[0, i, :, 0, i, :] = c
            table[0, i, :, 1, i, :] = sign * s
            table[1, i, :, 0, i, :] = -sign * s
            table[1, i, :, 1, i, :] = c
        return np.pad(table.reshape(160, 160), ((0, 0), (0, 96)))

    spread = np.zeros((2, 2, NG, 4, 128), np.float32)
    for group, steps in enumerate(STEPS_OF):
        for t, step in enumerate(steps):
            for half in range(2):
                spread[half, step, points, group, NG * t + points] = 1
    spread = spread.reshape(160, 512)
    parts = [first.reshape(240, 256), last.reshape(240, 256), rows(1.0), rows(-1.0), spread[:, :256], spread[:, 256:]]
    return np.concatenate(parts, 0).astype(ml_dtypes.bfloat16)


def matrix_from_flat(flat, matrix, odd):
    for a in range(NG // 2):
        for j in range(25):
            at = 128 * (25 * a + j)
            tile = flat[:, at : at + 128].astype(F32)
            if j <= 12:
                matrix[j, pl.ds(2 * a, 2, stride=NG), :] = tile
            if j >= 12:
                odd[j - 12, pl.ds(a, 2, stride=24), :] = tile
    lane = lax.broadcasted_iota(jnp.int32, (NG // 2, 128), 1)
    for c in range(2):
        here = pltpu.roll(odd[0, 24 * c : 24 * c + 20, :], 64, 1)
        for j in range(TILES):
            after = pltpu.roll(odd[j + 1, 24 * c : 24 * c + 20, :], 64, 1) if j < 12 else here
            matrix[j, pl.ds(NG * c + 1, 20, stride=2), :] = jnp.where(lane < 64, here, after)
            here = after


def flat_from_matrix(matrix, flat, odd, done):
    lane = lax.broadcasted_iota(jnp.int32, (NG // 2, 128), 1)
    for c in range(2):
        before = matrix[12, pl.ds(NG * c, 20, stride=2), :]
        for j in range(TILES):
            here = pltpu.roll(matrix[j, pl.ds(NG * c + 1, 20, stride=2), :], 64, 1)
            odd[j, 24 * c : 24 * c + 20, :] = jnp.where(lane < 64, before, here)
            before = here
    for a in range(NG // 2):
        for j in range(25):
            at = 128 * (25 * a + j)
            flat[:, at : at + 128] = (
                matrix[j, pl.ds(2 * a, 2, stride=NG), :] if j < 12 else odd[j - 12, pl.ds(a, 2, stride=24), :]
            )
        done(a)


def dot(a, b, on):
    return lax.dot_general(a, b, ((on[:1], on[1:]), ((), ())), preferred_element_type=F32)


def spread_coulomb(matrix, tab, out):
    for j in range(TILES):
        value = matrix[j]
        high = value.astype(BF16)
        low = (value - high.astype(F32)).astype(BF16)
        value = jnp.concatenate([high, low], 0)
        both = dot(value, tab[800:960, :], (0, 0))
        out[0, 128 * j : 128 * j + 128, :] = both[:, :128]
        out[1, 128 * j : 128 * j + 128, :] = both[:, 128:]
        out[2, 128 * j : 128 * j + 128, :] = dot(value, tab[960:1120, :128], (0, 0))


def terms(block, visiting, coulomb, tab, total, last, fa, fb, fc, fd):
    table = lambda at, rows, cols=256: tab[at : at + rows, :cols]
    rows = 2 * NG * len(visiting)
    for j in range(TILES):
        a = block[j].astype(F32)
        a_re, a_im = a[:NG], a[NG:]
        parts = []
        for ref in visiting:
            b = ref[j].astype(F32)
            b_re, b_im = b[:NG], b[NG:]
            parts += [a_re * b_re + a_im * b_im, a_im * b_re - a_re * b_im]
        density = jnp.concatenate(parts, 0).astype(BF16)
        fa[128 * j : 128 * j + 128, :] = dot(density, table(0, rows), (0, 0)).astype(BF16)
    forward, inverse = table(480, 160, 160), table(640, 160, 160)
    for i in range(10):
        at = 160 * i
        a, b = fa[at : at + 80, :], fa[at + 80 : at + 160, :]
        field = jnp.concatenate(
            [jnp.concatenate([a[:, :128], b[:, :128]], 1), jnp.concatenate([a[:, 128:], b[:, 128:]], 1)], 0
        )
        r = dot(forward, field, (1, 0))
        for c in range(2):
            fb[c, at : at + 80, :] = r[80 * c : 80 * c + 80, :128]
            fb[c, at + 80 : at + 160, :] = r[80 * c : 80 * c + 80, 128:]
    for i in range(10):
        halves, scales = [], []
        for h in range(2):
            z = 4 * i + 2 * h
            halves.append(
                jnp.concatenate([fb[c, pl.ds(z + q, NG, stride=NG), :] for c in range(2) for q in range(2)], 0)
            )
            scales.append(jnp.concatenate([coulomb[pl.ds(z + q, NG, stride=NG), :] for q in range(2)] * 2, 0))
        field = jnp.concatenate(halves, 1).astype(BF16)
        r = dot(forward, field, (1, 0)).astype(BF16).astype(F32)
        scaled = (r * jnp.concatenate(scales, 1)).astype(BF16)
        r = dot(inverse, scaled, (1, 0))
        for h in range(2):
            for c in range(2):
                for q in range(2):
                    at = 80 * c + NG * q
                    fc[c, pl.ds(4 * i + 2 * h + q, NG, stride=NG), :] = r[at : at + NG, 128 * h : 128 * h + 128]
    for i in range(10):
        at = 160 * i
        field = jnp.concatenate(
            [jnp.concatenate([fc[c, at : at + 80, :], fc[c, at + 80 : at + 160, :]], 1) for c in range(2)], 0
        ).astype(BF16)
        r = dot(inverse, field, (1, 0)).astype(BF16)
        fd[at : at + 80, :] = jnp.concatenate([r[:80, :128], r[80:, :128]], 1)
        fd[at + 80 : at + 160, :] = jnp.concatenate([r[:80, 128:], r[80:, 128:]], 1)
    for j in range(TILES):
        wave = dot(table(240, rows), fd[128 * j : 128 * j + 128, :], (1, 1))
        re = im = 0.0
        for t, ref in enumerate(visiting):
            b = ref[j].astype(F32)
            b_re, b_im = b[:NG], b[NG:]
            w_re, w_im = wave[80 * t : 80 * t + NG], wave[80 * t + NG : 80 * t + 80]
            re = re + (b_re * w_re - b_im * w_im)
            im = im + (b_re * w_im + b_im * w_re)
        value = jnp.concatenate([re, im], 0)
        total[j] = (total[j] + value) * WEIGHT if last else total[j] + value


def kernel(
    orbitals, coulomb, tables_ref, total,
    flat, kernel_flat, tab, matrix, kernel_matrix, odd, vis, passing, scale, fa, fb, fc, fd,
    local_sem, send_sem, recv_sem,
):
    n, k = lax.axis_index("band"), lax.axis_index("kpt")
    core = lax.rem(n, 2)
    sibling = n + 1 - 2 * core
    behind, ahead = lax.rem(n + NBLOCK - 2, NBLOCK), lax.rem(n + 2, NBLOCK)
    k_behind, k_ahead = lax.rem(k + NK - 1, NK), lax.rem(k + 1, NK)
    k_beside, k_corner = lax.rem(k + 4, NK), lax.rem(k + 3, NK)
    late, on_time = n < 2, n >= 2
    turns, turned = lax.rem(k, 4) == 3, lax.rem(k, 4) == 0

    barrier = pltpu.get_barrier_semaphore()

    def ready(*peers):
        for peer in peers:
            pl.semaphore_signal(barrier, inc=1, device_id=peer, device_id_type=MESH)

    ready((behind, k), (sibling, k))
    pl.when(jnp.logical_not(turned))(lambda: ready((n, k_behind)))
    pl.when(turned)(lambda: ready((n, k_corner), (n, k_beside), (behind, k_beside)))
    loads = [
        pltpu.make_async_copy(orbitals.at[0, 0], flat, local_sem.at[0]),
        pltpu.make_async_copy(coulomb.at[0], kernel_flat, local_sem.at[1]),
        pltpu.make_async_copy(tables_ref, tab, local_sem.at[2]),
    ]
    for load in loads:
        load.start()
    loads[0].wait()
    matrix_from_flat(flat, matrix, odd)
    vis[0] = matrix[:TILES].astype(BF16)
    pl.semaphore_wait(barrier, 3 + 2 * turned.astype(jnp.int32))

    used = [0]

    def copy(src, dst, peer, arrives=None):
        at = used[0]
        used[0] += 1
        arrives = at if arrives is None else arrives
        return pltpu.make_async_remote_copy(
            src_ref=src, dst_ref=dst, send_sem=send_sem.at[at], recv_sem=recv_sem.at[arrives],
            device_id=peer, device_id_type=MESH,
        )

    def chunk(ref, c):
        return ref.at[pl.ds(c[0], c[1])]

    def copies(src, dst, peer, arrives=None):
        arrives = (None, None) if arrives is None else (arrives, arrives + 1)
        return [copy(chunk(vis.at[src], c), chunk(vis.at[dst], c), peer, at) for c, at in zip(CHUNKS, arrives)]

    to_ahead = copies(0, 3, (ahead, k))
    to_next_k = copies(0, 1, (n, k_ahead), 24)
    on_x = copy(chunk(vis.at[1], CHUNKS[1]), chunk(vis.at[5], CHUNKS[1]), (ahead, k), 27)
    on_y = copy(chunk(vis.at[3], CHUNKS[0]), chunk(vis.at[5], CHUNKS[0]), (n, k_ahead), 26)
    round_y = [copy(chunk(vis.at[0], c), chunk(passing, c), (n, lax.rem(k + 5, NK))) for c in CHUNKS]
    pass_on = [
        copy(chunk(passing, c), chunk(vis.at[dst], c), peer, at + i)
        for i, c in enumerate(CHUNKS)
        for dst, peer, at in ((1, (n, k_beside), 24), (5, (ahead, k_beside), 26))
    ]
    even_own, even_partner = copies(0, 2, (sibling, k)), copies(1, 4, (sibling, k))
    odd_own, odd_partner = copies(3, 2, (sibling, k)), copies(5, 4, (sibling, k))

    def when(flag, *steps):
        @pl.when(flag)
        def _():
            for step in steps:
                step()

    def both(copies, name):
        return [getattr(c, name) for c in copies]

    straight, inner = jnp.logical_not(turns), jnp.logical_not(turned)
    when(turns, round_y[0].start)
    to_ahead[0].start()
    at_once = n >= NBLOCK - 2
    when(at_once, to_ahead[1].start)
    when(straight, to_next_k[1].start)
    when(core == 0, *both(even_own, "start"))
    total[:TILES] = jnp.zeros((TILES, 2 * NG, 128), F32)
    loads[1].wait()
    matrix_from_flat(kernel_flat, kernel_matrix, odd)
    loads[2].wait()
    spread_coulomb(kernel_matrix, tab, scale)
    when(turns, round_y[0].wait_send, round_y[1].start)
    when(straight, to_next_k[1].wait_send, to_next_k[0].start)
    when(jnp.logical_not(at_once), to_ahead[0].wait_send, to_ahead[1].start)
    @pl.when(turned)
    def _():
        terms(vis.at[0], [vis.at[0]], scale.at[0], tab, total, False, fa, fb, fc, fd)

    for i in range(2):
        when(turned, round_y[i].wait_recv, pass_on[2 * i + 1].start, pass_on[2 * i].start)

    def partner(i, flag):
        @pl.when(flag)
        def _():
            to_next_k[i].wait_recv()
            if i == 1:
                when(inner, on_x.start)
            when(core == 0, even_partner[i].start)

    def block_behind(i, flag):
        @pl.when(flag)
        def _():
            to_ahead[i].wait_recv()
            if i == 0:
                when(straight, on_y.start)
            when(core == 1, odd_own[i].start)

    early = turned | on_time

    def add(slots, steps, flag=None, last=False):
        def work():
            terms(vis.at[0], [vis.at[i] for i in slots], scale.at[steps], tab, total, last, fa, fb, fc, fd)

        work() if flag is None else pl.when(flag)(work)

    partner(1, inner)
    block_behind(0, early)
    partner(0, inner)
    block_behind(1, early)
    add((0, 1), 2, inner)
    block_behind(0, inner & late)
    block_behind(1, inner & late)
    when(core == 0, *both(odd_own, "wait_recv"))
    when(core == 1, *both(even_own, "wait_recv"))
    add((2, 3), 0)
    partner(0, turned)
    partner(1, turned)
    for i, arrived in enumerate((on_y, on_x)):
        arrived.wait_recv()
        when(core == 1, odd_partner[i].start)
    when(core == 0, *both(odd_partner, "wait_recv"))
    when(core == 1, *both(even_partner, "wait_recv"))
    add((4, 5), 1, inner, True)
    add((1, 4, 5), 1, turned, True)
    when(at_once, to_ahead[0].wait_send)
    to_ahead[1].wait_send()
    when(turns, round_y[1].wait_send)
    when(straight, to_next_k[0].wait_send, on_y.wait_send)
    when(inner, on_x.wait_send)
    when(turned, *both(pass_on, "wait_send"))
    when(core == 0, *both(even_own + even_partner, "wait_send"))
    when(core == 1, *both(odd_own + odd_partner, "wait_send"))


def write(total, out, odd, flat, sem):
    stores = [
        pltpu.make_async_copy(flat.at[:, pl.ds(at, 16000)], out.at[0, 0, :, pl.ds(at, 16000)], sem.at[i])
        for i, at in enumerate(range(0, 64000, 16000))
    ]

    def done(a):
        if a % 5 == 4:
            stores[a // 5].start()

    flat_from_matrix(total, flat, odd, done)
    for store in stores:
        store.wait()


def shards(orbitals, coulomb):
    field, spare = (TILES, 2 * NG, 128), (TILES + 4, 2 * NG, 128)
    vmem = pltpu.VMEM
    total = pl.pallas_call(
        kernel,
        out_shape=pltpu.VMEM(spare, F32),
        in_specs=[pl.BlockSpec(memory_space=pl.ANY)] * 3,
        out_specs=pl.BlockSpec(memory_space=pltpu.VMEM),
        scratch_shapes=[
            vmem((2, 64000), BF16), vmem((2, 64000), F32), vmem((1120, 256), BF16), vmem(spare, F32), vmem(spare, F32),
            vmem((TILES + 4, 48, 128), F32), vmem((6, *field), BF16), vmem(field, BF16), vmem((3, ROWS, 128), F32),
            vmem((ROWS, 256), BF16), vmem((2, 1600, 128), F32), vmem((2, 1600, 128), F32), vmem((ROWS, 256), BF16),
            pltpu.SemaphoreType.DMA((3,)), pltpu.SemaphoreType.DMA((24,)), pltpu.SemaphoreType.DMA((28,)),
        ],
        compiler_params=pltpu.CompilerParams(collective_id=0, has_side_effects=True, vmem_limit_bytes=56 << 20),
    )(orbitals, coulomb, jnp.asarray(tables()))
    return pl.pallas_call(
        write,
        out_shape=jax.ShapeDtypeStruct(orbitals.shape, F32),
        in_specs=[pl.BlockSpec(memory_space=pltpu.VMEM)],
        out_specs=pl.BlockSpec(memory_space=pl.ANY),
        scratch_shapes=[vmem((TILES + 4, 48, 128), F32), vmem((2, 64000), F32), pltpu.SemaphoreType.DMA((4,))],
        compiler_params=pltpu.CompilerParams(vmem_limit_bytes=16 << 20),
    )(total)


def solution(mesh):
    return jax.shard_map(
        shards,
        mesh=mesh,
        in_specs=(P("kpt", "band", None, None), P("kpt", None, None)),
        out_specs=P("kpt", "band", None, None),
        check_vma=False,
    )
```

```python
import math

import jax
import jax.numpy as jnp
import ml_dtypes
import numpy as np
from jax import lax
from jax.experimental import pallas as pl
from jax.experimental.pallas import tpu as pltpu
from jax.sharding import PartitionSpec as P

NG = 40
KSTEPS = 2
BSTEPS = 2
TERMS = BSTEPS + 1
STEPS_OF = ((0, 0, 0), (1, 1, 1), (0, 1, 1))
NBLOCK = 32
NK = 8
WEIGHT = -1.0 / (KSTEPS * TERMS)
BF16 = jnp.bfloat16
F32 = jnp.float32
MESH = pl.DeviceIdType.MESH
TILES = 13
ROWS = TILES * 128
CHUNKS = ((0, 5), (5, 8))


def tables():
    points = np.arange(NG)
    angle = (points[:, None] * points[None, :] % NG) * (2.0 * math.pi / NG)
    scale = 1.0 / math.sqrt(NG)
    c, s = (
        (f(angle) * scale).astype(ml_dtypes.bfloat16).astype(np.float32) for f in (np.cos, np.sin)
    )
    first = np.zeros((TERMS, 2, NG, 2, 128), np.float32)
    last = np.zeros((TERMS, 2, NG, 2, 128), np.float32)
    for t in range(TERMS):
        lanes = slice(NG * t, NG * t + NG)
        first[t, 0, :, 0, lanes] = c
        first[t, 1, :, 0, lanes] = s
        first[t, 0, :, 1, lanes] = -s
        first[t, 1, :, 1, lanes] = c
        last[t, 0, :, 0, lanes] = c
        last[t, 0, :, 1, lanes] = -s
        last[t, 1, :, 1, lanes] = c
        last[t, 1, :, 0, lanes] = s

    def rows(sign):
        table = np.zeros((2, 2, NG, 2, 2, NG), np.float32)
        for i in range(2):
            table[0, i, :, 0, i, :] = c
            table[0, i, :, 1, i, :] = sign * s
            table[1, i, :, 0, i, :] = -sign * s
            table[1, i, :, 1, i, :] = c
        return np.pad(table.reshape(160, 160), ((0, 0), (0, 96)))

    spread = np.zeros((2, 2, NG, 4, 128), np.float32)
    for group, steps in enumerate(STEPS_OF):
        for t, step in enumerate(steps):
            for half in range(2):
                spread[half, step, points, group, NG * t + points] = 1
    spread = spread.reshape(160, 512)
    parts = [first.reshape(240, 256), last.reshape(240, 256), rows(1.0), rows(-1.0), spread[:, :256], spread[:, 256:]]
    return np.concatenate(parts, 0).astype(ml_dtypes.bfloat16)


def matrix_from_flat(flat, matrix, odd):
    for a in range(NG // 2):
        for j in range(25):
            at = 128 * (25 * a + j)
            tile = flat[:, at : at + 128].astype(F32)
            if j <= 12:
                matrix[j, pl.ds(2 * a, 2, stride=NG), :] = tile
            if j >= 12:
                odd[j - 12, pl.ds(a, 2, stride=24), :] = tile
    lane = lax.broadcasted_iota(jnp.int32, (NG // 2, 128), 1)
    for c in range(2):
        here = pltpu.roll(odd[0, 24 * c : 24 * c + 20, :], 64, 1)
        for j in range(TILES):
            after = pltpu.roll(odd[j + 1, 24 * c : 24 * c + 20, :], 64, 1) if j < 12 else here
            matrix[j, pl.ds(NG * c + 1, 20, stride=2), :] = jnp.where(lane < 64, here, after)
            here = after


def flat_from_matrix(matrix, flat, odd, done):
    lane = lax.broadcasted_iota(jnp.int32, (NG // 2, 128), 1)
    for c in range(2):
        before = matrix[12, pl.ds(NG * c, 20, stride=2), :]
        for j in range(TILES):
            here = pltpu.roll(matrix[j, pl.ds(NG * c + 1, 20, stride=2), :], 64, 1)
            odd[j, 24 * c : 24 * c + 20, :] = jnp.where(lane < 64, before, here)
            before = here
    for a in range(NG // 2):
        for j in range(25):
            at = 128 * (25 * a + j)
            flat[:, at : at + 128] = (
                matrix[j, pl.ds(2 * a, 2, stride=NG), :] if j < 12 else odd[j - 12, pl.ds(a, 2, stride=24), :]
            )
        done(a)


def dot(a, b, on):
    return lax.dot_general(a, b, ((on[:1], on[1:]), ((), ())), preferred_element_type=F32)


def spread_coulomb(matrix, tab, out):
    for j in range(TILES):
        value = matrix[j]
        high = value.astype(BF16)
        low = (value - high.astype(F32)).astype(BF16)
        value = jnp.concatenate([high, low], 0)
        both = dot(value, tab[800:960, :], (0, 0))
        out[0, 128 * j : 128 * j + 128, :] = both[:, :128]
        out[1, 128 * j : 128 * j + 128, :] = both[:, 128:]
        out[2, 128 * j : 128 * j + 128, :] = dot(value, tab[960:1120, :128], (0, 0))


def terms(block, visiting, coulomb, tab, total, last, fa, fb, fc, fd):
    table = lambda at, rows, cols=256: tab[at : at + rows, :cols]
    rows = 2 * NG * len(visiting)
    for j in range(TILES):
        a = block[j].astype(F32)
        a_re, a_im = a[:NG], a[NG:]
        parts = []
        for ref in visiting:
            b = ref[j].astype(F32)
            b_re, b_im = b[:NG], b[NG:]
            parts += [a_re * b_re + a_im * b_im, a_im * b_re - a_re * b_im]
        density = jnp.concatenate(parts, 0).astype(BF16)
        fa[128 * j : 128 * j + 128, :] = dot(density, table(0, rows), (0, 0)).astype(BF16)
    forward, inverse = table(480, 160, 160), table(640, 160, 160)
    for i in range(10):
        at = 160 * i
        a, b = fa[at : at + 80, :], fa[at + 80 : at + 160, :]
        field = jnp.concatenate(
            [jnp.concatenate([a[:, :128], b[:, :128]], 1), jnp.concatenate([a[:, 128:], b[:, 128:]], 1)], 0
        )
        r = dot(forward, field, (1, 0))
        for c in range(2):
            fb[c, at : at + 80, :] = r[80 * c : 80 * c + 80, :128]
            fb[c, at + 80 : at + 160, :] = r[80 * c : 80 * c + 80, 128:]
    for i in range(10):
        halves, scales = [], []
        for h in range(2):
            z = 4 * i + 2 * h
            halves.append(
                jnp.concatenate([fb[c, pl.ds(z + q, NG, stride=NG), :] for c in range(2) for q in range(2)], 0)
            )
            scales.append(jnp.concatenate([coulomb[pl.ds(z + q, NG, stride=NG), :] for q in range(2)] * 2, 0))
        field = jnp.concatenate(halves, 1).astype(BF16)
        r = dot(forward, field, (1, 0)).astype(BF16).astype(F32)
        scaled = (r * jnp.concatenate(scales, 1)).astype(BF16)
        r = dot(inverse, scaled, (1, 0))
        for h in range(2):
            for c in range(2):
                for q in range(2):
                    at = 80 * c + NG * q
                    fc[c, pl.ds(4 * i + 2 * h + q, NG, stride=NG), :] = r[at : at + NG, 128 * h : 128 * h + 128]
    for i in range(10):
        at = 160 * i
        field = jnp.concatenate(
            [jnp.concatenate([fc[c, at : at + 80, :], fc[c, at + 80 : at + 160, :]], 1) for c in range(2)], 0
        ).astype(BF16)
        r = dot(inverse, field, (1, 0)).astype(BF16)
        fd[at : at + 80, :] = jnp.concatenate([r[:80, :128], r[80:, :128]], 1)
        fd[at + 80 : at + 160, :] = jnp.concatenate([r[:80, 128:], r[80:, 128:]], 1)
    for j in range(TILES):
        wave = dot(table(240, rows), fd[128 * j : 128 * j + 128, :], (1, 1))
        re = im = 0.0
        for t, ref in enumerate(visiting):
            b = ref[j].astype(F32)
            b_re, b_im = b[:NG], b[NG:]
            w_re, w_im = wave[80 * t : 80 * t + NG], wave[80 * t + NG : 80 * t + 80]
            re = re + (b_re * w_re - b_im * w_im)
            im = im + (b_re * w_im + b_im * w_re)
        value = jnp.concatenate([re, im], 0)
        total[j] = (total[j] + value) * WEIGHT if last else total[j] + value


def kernel(
    orbitals, coulomb, tables_ref, total,
    flat, kernel_flat, tab, matrix, kernel_matrix, odd, vis, passing, scale, fa, fb, fc, fd,
    local_sem, send_sem, recv_sem,
):
    n, k = lax.axis_index("band"), lax.axis_index("kpt")
    core = lax.rem(n, 2)
    sibling = n + 1 - 2 * core
    behind, ahead = lax.rem(n + NBLOCK - 2, NBLOCK), lax.rem(n + 2, NBLOCK)
    k_behind, k_ahead = lax.rem(k + NK - 1, NK), lax.rem(k + 1, NK)
    k_beside, k_corner = lax.rem(k + 4, NK), lax.rem(k + 3, NK)
    late, on_time = n < 2, n >= 2
    turns, turned = lax.rem(k, 4) == 3, lax.rem(k, 4) == 0

    barrier = pltpu.get_barrier_semaphore()

    def ready(*peers):
        for peer in peers:
            pl.semaphore_signal(barrier, inc=1, device_id=peer, device_id_type=MESH)

    ready((behind, k), (sibling, k))
    pl.when(jnp.logical_not(turned))(lambda: ready((n, k_behind)))
    pl.when(turned)(lambda: ready((n, k_corner), (n, k_beside), (behind, k_beside)))
    loads = [
        pltpu.make_async_copy(orbitals.at[0, 0], flat, local_sem.at[0]),
        pltpu.make_async_copy(coulomb.at[0], kernel_flat, local_sem.at[1]),
        pltpu.make_async_copy(tables_ref, tab, local_sem.at[2]),
    ]
    for load in loads:
        load.start()
    loads[0].wait()
    matrix_from_flat(flat, matrix, odd)
    vis[0] = matrix[:TILES].astype(BF16)
    pl.semaphore_wait(barrier, 3 + 2 * turned.astype(jnp.int32))

    used = [0]

    def copy(src, dst, peer, arrives=None):
        at = used[0]
        used[0] += 1
        arrives = at if arrives is None else arrives
        return pltpu.make_async_remote_copy(
            src_ref=src, dst_ref=dst, send_sem=send_sem.at[at], recv_sem=recv_sem.at[arrives],
            device_id=peer, device_id_type=MESH,
        )

    def chunk(ref, c):
        return ref.at[pl.ds(c[0], c[1])]

    def copies(src, dst, peer, arrives=None):
        arrives = (None, None) if arrives is None else (arrives, arrives + 1)
        return [copy(chunk(vis.at[src], c), chunk(vis.at[dst], c), peer, at) for c, at in zip(CHUNKS, arrives)]

    to_ahead = copies(0, 3, (ahead, k))
    to_next_k = copies(0, 1, (n, k_ahead), 24)
    on_x = copy(chunk(vis.at[1], CHUNKS[1]), chunk(vis.at[5], CHUNKS[1]), (ahead, k), 27)
    on_y = copy(chunk(vis.at[3], CHUNKS[0]), chunk(vis.at[5], CHUNKS[0]), (n, k_ahead), 26)
    round_y = [copy(chunk(vis.at[0], c), chunk(passing, c), (n, lax.rem(k + 5, NK))) for c in CHUNKS]
    pass_on = [
        copy(chunk(passing, c), chunk(vis.at[dst], c), peer, at + i)
        for i, c in enumerate(CHUNKS)
        for dst, peer, at in ((1, (n, k_beside), 24), (5, (ahead, k_beside), 26))
    ]
    even_own, even_partner = copies(0, 2, (sibling, k)), copies(1, 4, (sibling, k))
    odd_own, odd_partner = copies(3, 2, (sibling, k)), copies(5, 4, (sibling, k))

    def when(flag, *steps):
        @pl.when(flag)
        def _():
            for step in steps:
                step()

    def both(copies, name):
        return [getattr(c, name) for c in copies]

    straight, inner = jnp.logical_not(turns), jnp.logical_not(turned)
    when(turns, round_y[0].start)
    to_ahead[0].start()
    at_once = n >= NBLOCK - 2
    when(at_once, to_ahead[1].start)
    when(straight, to_next_k[1].start)
    when(core == 0, *both(even_own, "start"))
    total[:TILES] = jnp.zeros((TILES, 2 * NG, 128), F32)
    loads[1].wait()
    matrix_from_flat(kernel_flat, kernel_matrix, odd)
    when(turns, round_y[0].wait_send, round_y[1].start)
    when(straight, to_next_k[1].wait_send, to_next_k[0].start)
    when(jnp.logical_not(at_once), to_ahead[0].wait_send, to_ahead[1].start)
    loads[2].wait()
    spread_coulomb(kernel_matrix, tab, scale)
    @pl.when(turned)
    def _():
        terms(vis.at[0], [vis.at[0]], scale.at[0], tab, total, False, fa, fb, fc, fd)

    for i in range(2):
        when(turned, round_y[i].wait_recv, pass_on[2 * i + 1].start, pass_on[2 * i].start)

    def partner(i, flag):
        @pl.when(flag)
        def _():
            to_next_k[i].wait_recv()
            if i == 1:
                when(inner, on_x.start)
            when(core == 0, even_partner[i].start)

    def block_behind(i, flag):
        @pl.when(flag)
        def _():
            to_ahead[i].wait_recv()
            if i == 0:
                when(straight, on_y.start)
            when(core == 1, odd_own[i].start)

    early = turned | on_time

    def add(slots, steps, flag=None, last=False):
        def work():
            terms(vis.at[0], [vis.at[i] for i in slots], scale.at[steps], tab, total, last, fa, fb, fc, fd)

        work() if flag is None else pl.when(flag)(work)

    partner(1, inner)
    block_behind(0, early)
    partner(0, inner)
    block_behind(1, early)
    add((0, 1), 2, inner)
    block_behind(0, inner & late)
    block_behind(1, inner & late)
    when(core == 0, *both(odd_own, "wait_recv"))
    when(core == 1, *both(even_own, "wait_recv"))
    add((2, 3), 0)
    partner(0, turned)
    partner(1, turned)
    for i, arrived in enumerate((on_y, on_x)):
        arrived.wait_recv()
        when(core == 1, odd_partner[i].start)
    when(core == 0, *both(odd_partner, "wait_recv"))
    when(core == 1, *both(even_partner, "wait_recv"))
    add((4, 5), 1, inner, True)
    add((1, 4, 5), 1, turned, True)
    when(at_once, to_ahead[0].wait_send)
    to_ahead[1].wait_send()
    when(turns, round_y[1].wait_send)
    when(straight, to_next_k[0].wait_send, on_y.wait_send)
    when(inner, on_x.wait_send)
    when(turned, *both(pass_on, "wait_send"))
    when(core == 0, *both(even_own + even_partner, "wait_send"))
    when(core == 1, *both(odd_own + odd_partner, "wait_send"))


def write(total, out, odd, flat, sem):
    stores = [
        pltpu.make_async_copy(flat.at[:, pl.ds(at, 16000)], out.at[0, 0, :, pl.ds(at, 16000)], sem.at[i])
        for i, at in enumerate(range(0, 64000, 16000))
    ]

    def done(a):
        if a % 5 == 4:
            stores[a // 5].start()

    flat_from_matrix(total, flat, odd, done)
    for store in stores:
        store.wait()


def shards(orbitals, coulomb):
    field, spare = (TILES, 2 * NG, 128), (TILES + 4, 2 * NG, 128)
    vmem = pltpu.VMEM
    total = pl.pallas_call(
        kernel,
        out_shape=pltpu.VMEM(spare, F32),
        in_specs=[pl.BlockSpec(memory_space=pl.ANY)] * 3,
        out_specs=pl.BlockSpec(memory_space=pltpu.VMEM),
        scratch_shapes=[
            vmem((2, 64000), BF16), vmem((2, 64000), F32), vmem((1120, 256), BF16), vmem(spare, F32), vmem(spare, F32),
            vmem((TILES + 4, 48, 128), F32), vmem((6, *field), BF16), vmem(field, BF16), vmem((3, ROWS, 128), F32),
            vmem((ROWS, 256), BF16), vmem((2, 1600, 128), F32), vmem((2, 1600, 128), F32), vmem((ROWS, 256), BF16),
            pltpu.SemaphoreType.DMA((3,)), pltpu.SemaphoreType.DMA((24,)), pltpu.SemaphoreType.DMA((28,)),
        ],
        compiler_params=pltpu.CompilerParams(collective_id=0, has_side_effects=True, vmem_limit_bytes=56 << 20),
    )(orbitals, coulomb, jnp.asarray(tables()))
    return pl.pallas_call(
        write,
        out_shape=jax.ShapeDtypeStruct(orbitals.shape, F32),
        in_specs=[pl.BlockSpec(memory_space=pltpu.VMEM)],
        out_specs=pl.BlockSpec(memory_space=pl.ANY),
        scratch_shapes=[vmem((TILES + 4, 48, 128), F32), vmem((2, 64000), F32), pltpu.SemaphoreType.DMA((4,))],
        compiler_params=pltpu.CompilerParams(vmem_limit_bytes=16 << 20),
    )(total)


def solution(mesh):
    return jax.shard_map(
        shards,
        mesh=mesh,
        in_specs=(P("kpt", "band", None, None), P("kpt", None, None)),
        out_specs=P("kpt", "band", None, None),
        check_vma=False,
    )
```
